32 devices in a mesh: groups: 2 (over y), ctx: 4 (over z), exp: 2 (over x), tp: 2 (over core).
Axes of the slice: x: 2, y: 2, z: 4, core: 2. Of those that a mesh axis runs over, the one named last changes fastest.
Arguments:
- query_rows: bfloat16 [1024, 3072], P(('groups', 'ctx'), ('exp', 'tp')), parts along dimension 0, may hold values from -8 to 8
- key_rows: bfloat16 [1024, 512], P(('groups', 'ctx'), 'exp'), parts along dimension 0, may hold values from -8 to 8
- value_rows: bfloat16 [1024, 512], P(('groups', 'ctx'), 'exp'), parts along dimension 0, may hold values from -6 to 6
- residual: bfloat16 [1024, 3072], P(('groups', 'ctx'), ('exp', 'tp')), parts along dimension 0, may hold values from -4 to 4
- norm_gain: float32 [3072], P(('exp', 'tp')), may hold values from 0.5 to 1.5
- router_weight: float32 [3072, 8], P(('exp', 'tp')), may hold values from -0.109375 to 0.109375
- expert_ids: int32 [1024, 2], P(('groups', 'ctx')), parts along dimension 0, may hold values from 0 to 7, all different within a row; in each aligned block of 128 rows (0 to 127, 128 to 255, ...) at most 48 rows name the same one
- gate_weight: bfloat16 [3072, 2, 32768], P('exp', 'tp', 'ctx'), may hold values from -0.109375 to 0.109375
- down_weight: bfloat16 [2, 32768, 3072], P('tp', 'ctx', 'exp'), may hold values from -0.0625 to 0.0625
Outputs:
- layer_out: bfloat16 [1024, 3072], P(('groups', 'ctx'), ('exp', 'tp')), parts along dimension 0
The draws below stay inside these ranges and needn't reach their ends.
There are 2 independent parts, one for each index of `groups`. The reference program is written for one: setup_inputs(seed, part) draws one part's arguments, and reference() takes and returns one part's arrays. A program takes and returns all parts, laid end to end along the dimension named above; an argument that names none is the same for every part. Nothing has to cross between parts.
Inputs may be any that keep to these rules, and one draw needn't show every extreme that they name: `expert_ids`: each token names two different experts; among the 128 tokens of each aligned block no expert is named more than 48 times.
All inputs are finite; a program needn't handle non-finite values.
Results may differ from the reference program's by a relative error of at most 0.012.
Values may be sent and summed in bfloat16 or wider, within the bound.
A program may use at most 192 MiB of HBM per device.

```python
import math
import jax
import jax.numpy as jnp
import numpy as np
from jax import lax

HD = 128
QH = 24
KVH = 4
E = 8
FF = 8192
LOC = 128
D = 3072
C = 48
TOKENS = 512
TP_WAYS = 2
SPLIT_COLS = 32768
N_EXP = 2


def draw_query_rows(key, part):
    key = jax.random.fold_in(key, 11)
    drawn = jnp.clip(jax.random.normal(key, (TOKENS, KVH, QH // KVH, HD), jnp.float32), -6.0, 6.0)
    return drawn.reshape(TOKENS, QH * HD).astype(jnp.bfloat16)


def draw_key_rows(key, part):
    key = jax.random.fold_in(key, 12)
    drawn = jnp.clip(jax.random.normal(key, (TOKENS, KVH, HD), jnp.float32), -6.0, 6.0)
    return drawn.reshape(TOKENS, KVH * HD).astype(jnp.bfloat16)


def steps_of(key, dims, split, smallest, largest):
    loudness = 1.0
    for dim, parts in split:
        steps = jax.random.uniform(jax.random.fold_in(jax.random.fold_in(key, 6), dim), (parts,), jnp.float32, smallest / len(split), largest / len(split))
        loudness = loudness * jnp.repeat(jnp.exp(steps), dims[dim] // parts).reshape((-1,) + (1,) * (len(dims) - 1 - dim))
    return loudness


def assign_block(rng, own, number, rows, amount, top, reach, lean):
    ranking = jax.random.permutation(rng, amount)
    heavy_load, common = shares(amount, rows * top, reach, lean, True), shares(amount, rows * top, reach, lean, False)
    places = jnp.arange(amount)

    def named(lengths, turn):
        used = int((lengths > 0).sum())
        fixed = max(1, used // 4)
        shifted = fixed + (places - fixed + turn * (used - fixed)) % max(1, amount - fixed)
        return jnp.zeros((amount,), jnp.int32).at[ranking[jnp.where(places < fixed, places, shifted)]].set(jnp.asarray(lengths, jnp.int32))

    lengths = jnp.where(number % 4 == 0, named(heavy_load, number // 4), named(common, number - number // 4 - 1))
    mixed = jax.random.permutation(jax.random.fold_in(own, 3), amount)
    donor, taker = mixed[0:amount // 2 * 2:2], mixed[1:amount // 2 * 2:2]
    margin = jnp.minimum(lengths[donor] - 1, reach - lengths[taker]) // 2
    margin = jnp.where((donor == ranking[0]) | (taker == ranking[0]) | (lengths[taker] == 0), 0, jnp.maximum(margin, 0))
    shifted = jax.random.randint(jax.random.fold_in(own, 4), (amount // 2,), 0, 1 << 20) % (margin + 1)
    lengths = lengths.at[donor].add(-shifted).at[taker].add(shifted)
    members = jnp.searchsorted(jnp.cumsum(lengths), jnp.arange(rows * top), side="right").astype(jnp.int32)
    table = members.reshape(top, rows).T
    table = table[jax.random.permutation(jax.random.fold_in(own, 1), rows)]
    turn = jax.random.randint(jax.random.fold_in(own, 2), (rows, 1), 0, top)
    return jnp.take_along_axis(table, (jnp.arange(top)[None, :] + turn) % top, axis=1)


def shares(count, total, most, lean, full):
    weights = [(1 << 20) // math.isqrt(rank ** lean) + 1 for rank in range(1, count + 1)]
    largest = most if full else min(most, max(-(-total // count), total * weights[0] // sum(weights)))
    least = 1 if total - largest >= count - 1 else 0
    counts, surplus = [largest] + [least] * (count - 1), total - largest - least * (count - 1)
    while surplus > 0:
        free = [i for i in range(1, count) if counts[i] < largest] or [i for i in range(1, count) if counts[i] < most]
        whole, budget = sum([weights[i] for i in free]), surplus
        for i in free:
            more = min(most - counts[i], max(1, budget * weights[i] // whole), surplus)
            counts[i] = counts[i] + more
            surplus = surplus - more
    return np.array(counts)


def centred(own_key, dims, spread, limit, cuts=(), kind=jnp.bfloat16):
    entries = spread * jax.random.normal(own_key, dims, jnp.float32)
    if cuts:
        entries = entries * steps_of(own_key, dims, cuts, -0.22, 0.18)
    return jnp.clip(entries, -limit, limit).astype(kind)


def setup_inputs(seed: int = 0, part: int = 0) -> dict:
    key_of = jax.random.split(jax.random.key(seed), 10)
    part_splits = jax.random.split(jax.random.fold_in(key_of[9], part), 10)
    query_rows = draw_query_rows(jax.random.fold_in(jax.random.fold_in(key_of[9], part), 71), part)
    key_rows = draw_key_rows(jax.random.fold_in(jax.random.fold_in(key_of[9], part), 71), part)
    value_rows = centred(part_splits[2], (TOKENS, KVH * HD), 1.0, 6.0, ((0, 4), (1, 2)))
    residual = centred(part_splits[3], (TOKENS, D), 0.5, 4.0, ((0, 4), (1, 4)))
    norm_gain = jnp.clip(1.0 + 0.1 * jax.random.normal(key_of[4], (D,), jnp.float32), 0.5, 1.5)
    router_weight = centred(key_of[5], (D, E), D ** -0.5, 0.109375, ((0, 4),), jnp.float32)
    expert_ids_keys = jax.random.split(jax.random.fold_in(part_splits[6], 1), TOKENS // LOC)
    expert_ids_turns = jax.random.permutation(jax.random.fold_in(part_splits[6], 3), TOKENS // LOC)
    expert_ids = jax.vmap(lambda own, number: assign_block(jax.random.fold_in(part_splits[6], 2), own, number, LOC, E, 2, C, 2))(expert_ids_keys, expert_ids_turns).reshape((TOKENS, 2))
    gate_weight = centred(key_of[7], (D, TP_WAYS, SPLIT_COLS), D ** -0.5, 0.109375, ((0, 2), (1, 2), (2, 4)))
    down_weight = centred(key_of[8], (TP_WAYS, SPLIT_COLS, D), FF ** -0.5, 0.0625, ((0, 2), (1, 4), (2, 2)))
    return dict(query_rows=query_rows, key_rows=key_rows, value_rows=value_rows, residual=residual, norm_gain=norm_gain, router_weight=router_weight, expert_ids=expert_ids, gate_weight=gate_weight, down_weight=down_weight)


epsilon = 1e-05
highest = lax.Precision.HIGHEST

def attention(query_rows, key_rows, value_rows):
    tokens = query_rows.shape[0]
    group_size = QH // KVH
    query_heads = jnp.transpose(query_rows.reshape(tokens, KVH, group_size, HD), (1, 0, 2, 3))
    key_heads = jnp.transpose(key_rows.reshape(tokens, KVH, HD), (1, 0, 2))
    value_heads = jnp.transpose(value_rows.reshape(tokens, KVH, HD), (1, 0, 2))
    position = jnp.arange(tokens, dtype=jnp.int32)
    causal = position[:, None] >= position[None, :]

    def one_head(operands):
        query_part, key_part, value_part = operands
        scores = jnp.einsum('tgd,sd->gts', query_part.astype(jnp.float32), key_part.astype(jnp.float32), precision=highest) * (1.0 / math.sqrt(HD))
        scores = jnp.where(causal[None], scores, -jnp.inf)
        weights = jax.nn.softmax(scores, axis=-1)
        return jnp.einsum('gts,sd->tgd', weights, value_part.astype(jnp.float32), precision=highest)
    head_out = lax.map(one_head, (query_heads, key_heads, value_heads))
    return jnp.transpose(head_out, (1, 0, 2, 3)).reshape(tokens, QH * HD)

def expert_stacks(gate_weight, down_weight):
    gate_stack = gate_weight.reshape(D, TP_WAYS, E, FF // TP_WAYS)
    gate_stack = jnp.transpose(gate_stack, (2, 0, 1, 3)).reshape(E, D, FF)
    down_stack = down_weight.reshape(TP_WAYS, E, FF // TP_WAYS, D)
    down_stack = jnp.transpose(down_stack, (1, 0, 2, 3)).reshape(E, FF, D)
    return (gate_stack, down_stack)

def reference(query_rows, key_rows, value_rows, residual, norm_gain, router_weight, expert_ids, gate_weight, down_weight):
    attended = attention(query_rows, key_rows, value_rows)
    mixed_in = residual.astype(jnp.float32) + attended
    inv_rms = lax.rsqrt(lax.optimization_barrier(jnp.mean(mixed_in * mixed_in, axis=1, keepdims=True)) + epsilon)
    normed = mixed_in * inv_rms * norm_gain[None, :]
    moe_input = normed.astype(jnp.bfloat16)
    logits = jnp.dot(normed, router_weight, precision=highest)
    picked = jnp.take_along_axis(logits, expert_ids, axis=1)
    first_gate = jax.nn.sigmoid(picked[:, 0] - picked[:, 1])
    second_gate = jax.nn.sigmoid(picked[:, 1] - picked[:, 0])
    gate_pair = jnp.stack([first_gate, second_gate], axis=1)
    blocks = TOKENS // LOC
    flat_ids = expert_ids.reshape(blocks, LOC * 2)
    flat_hot = (flat_ids[:, :, None] == jnp.arange(E, dtype=jnp.int32)[None, None, :]).astype(jnp.int32)
    slot_index = lax.optimization_barrier(jnp.sum((jnp.cumsum(flat_hot, axis=1) - flat_hot) * flat_hot, axis=2))
    buffer_row = jnp.arange(blocks, dtype=jnp.int32)[:, None] * C + slot_index
    token_index = jnp.arange(blocks, dtype=jnp.int32)[:, None] * LOC + jnp.arange(LOC * 2, dtype=jnp.int32)[None, :] // 2
    buffer = jnp.zeros((E, blocks * C, D), jnp.bfloat16).at[flat_ids, buffer_row].set(moe_input[token_index])
    gate_stack, down_stack = expert_stacks(gate_weight, down_weight)
    block_width = D // N_EXP

    def one_expert(operands):
        expert_input, gate_part, down_part = operands
        pre_act = jnp.zeros((expert_input.shape[0], FF), jnp.float32)
        for block_index in range(N_EXP):
            low = block_index * block_width
            block_term = jnp.dot(expert_input[:, low:low + block_width], gate_part[low:low + block_width], preferred_element_type=jnp.float32)
            block_term = lax.optimization_barrier(block_term.astype(jnp.bfloat16)).astype(jnp.float32)
            pre_act = pre_act + block_term
        hidden = jax.nn.silu(pre_act).astype(jnp.bfloat16)
        return jnp.dot(hidden, down_part, preferred_element_type=jnp.float32)
    outputs = lax.map(one_expert, (buffer, gate_stack, down_stack))
    picked_rows = outputs[flat_ids, buffer_row]
    expert_sum = lax.optimization_barrier(jnp.sum(picked_rows.reshape(TOKENS, 2, D) * gate_pair[:, :, None], axis=1))
    return (mixed_in + expert_sum).astype(jnp.bfloat16)
```

```python
import math

import jax
import jax.numpy as jnp
from jax import lax
from jax.sharding import PartitionSpec as P

HD = 128
QH = 24
KVH = 4
E = 8
C = 48
PIECES = 2


epsilon = 1e-05
highest = lax.Precision.HIGHEST
floor_score = -1e30


def per_device(
    query_rows,
    key_rows,
    value_rows,
    residual,
    norm_gain,
    router_weight,
    expert_ids,
    gate_weight,
    down_weight,
):
    ctx_count = lax.axis_size("ctx")
    exp_count = lax.axis_size("exp")
    tp_count = lax.axis_size("tp")
    tp_index = lax.axis_index("tp")
    row_count = query_rows.shape[0]
    kv_local = key_rows.shape[1] // HD
    query_local = query_rows.shape[1] // HD
    group_size = QH // KVH
    assert group_size % query_local == 0 and tp_count == 2
    owner = (tp_index * query_local) // group_size
    first_row = lax.axis_index("ctx") * row_count
    query_pos = first_row + jnp.arange(row_count, dtype=jnp.int32)
    query_heads = query_rows.reshape(row_count, query_local, HD)

    def own_head(rows):
        return lax.dynamic_slice_in_dim(rows, owner * HD, HD, axis=1)

    pair = jnp.concatenate([own_head(key_rows), own_head(value_rows)], axis=1)
    pair = lax.all_gather(pair, "ctx", axis=0, tiled=True)
    key_head, value_head = pair[:, :HD], pair[:, HD:]
    visible = query_pos[:, None] >= jnp.arange(pair.shape[0], dtype=jnp.int32)[None, :]
    scores = jnp.einsum(
        "tqd,sd->qts", query_heads, key_head, preferred_element_type=jnp.float32
    ) * (1.0 / math.sqrt(HD))
    scores = jnp.where(visible[None], scores, floor_score)
    weights = jnp.exp(scores - jnp.max(scores, axis=-1, keepdims=True))
    run_total = jnp.sum(weights, axis=-1, keepdims=True)
    accumulated = jnp.einsum(
        "qts,sd->qtd",
        weights.astype(jnp.bfloat16),
        value_head,
        preferred_element_type=jnp.float32,
    )
    attended = jnp.transpose(accumulated / run_total, (1, 0, 2)).reshape(row_count, -1)
    mixed_in = residual.astype(jnp.float32) + attended
    scaled = mixed_in * norm_gain[None, :]
    square_sum, logit_part = lax.psum(
        (jnp.sum(mixed_in * mixed_in, axis=1), jnp.dot(scaled, router_weight, precision=highest)),
        ("exp", "tp"),
    )
    inv_rms = lax.rsqrt(square_sum / (QH * HD) + epsilon)
    moe_half = (scaled * inv_rms[:, None]).astype(jnp.bfloat16)
    logits = logit_part * inv_rms[:, None]
    expert_range = jnp.arange(E, dtype=jnp.int32)
    chosen_hot = expert_ids[:, :, None] == expert_range[None, None, :]
    picked = jnp.sum(jnp.where(chosen_hot, logits[:, None, :], 0.0), axis=2)
    gate_pair = jnp.stack(
        [jax.nn.sigmoid(picked[:, 0] - picked[:, 1]), jax.nn.sigmoid(picked[:, 1] - picked[:, 0])],
        axis=1,
    )
    flat_ids = expert_ids.reshape(-1)
    flat_hot = (flat_ids[:, None] == expert_range[None, :]).astype(jnp.int32)
    slot_index = jnp.sum((jnp.cumsum(flat_hot, axis=0) - flat_hot) * flat_hot, axis=1)
    tile_row = (flat_ids * C + slot_index).reshape(row_count, 2)
    tile_range = jnp.arange(E * C, dtype=jnp.int32)
    tile_hot = tile_row[:, :, None] == tile_range[None, None, :]
    combine_matrix = jnp.sum(jnp.where(tile_hot, gate_pair[:, :, None], 0.0), axis=1)
    dispatch_matrix = jnp.transpose(jnp.any(tile_hot, axis=1)).astype(jnp.bfloat16)
    ctx_sharing = max(1, ctx_count // E)
    experts_held = max(1, E // ctx_count)
    send_tiles = jnp.dot(dispatch_matrix, moe_half, preferred_element_type=jnp.float32).astype(
        jnp.bfloat16
    )
    send_tiles = send_tiles.reshape(E, C, -1)
    outgoing = jnp.repeat(send_tiles, ctx_sharing, axis=0).reshape(ctx_count, experts_held, C, -1)
    hidden_width = gate_weight.shape[2] // experts_held
    pieces = max(1, min(PIECES, hidden_width // 512))
    piece = hidden_width // pieces
    arrived = []
    for e in range(experts_held):
        half = lax.all_to_all(outgoing[:, e], "ctx", split_axis=0, concat_axis=0, tiled=True)
        arrived.append(
            lax.all_gather(half.reshape(ctx_count * C, -1), "tp", axis=1, tiled=True)
        )
    sums = []
    for e in range(experts_held):
        for i in range(pieces):
            low = e * hidden_width + i * piece
            part = jnp.dot(
                arrived[e],
                gate_weight[:, 0, low : low + piece],
                preferred_element_type=jnp.float32,
            ).astype(jnp.bfloat16)
            total = part.astype(jnp.float32)
            for shift in range(1, exp_count):
                turned = [(j, (j + shift) % exp_count) for j in range(exp_count)]
                total = total + lax.ppermute(part, "exp", turned).astype(jnp.float32)
            sums.append(total)
    width_out = down_weight.shape[2] // tp_count
    moe_mine = 0.0
    combine_parts = combine_matrix.reshape(row_count, -1, experts_held, C)
    for e in range(experts_held):
        out = 0.0
        for i in range(pieces):
            low = e * hidden_width + i * piece
            hidden = jax.nn.silu(sums[e * pieces + i]).astype(jnp.bfloat16)
            out = out + jnp.dot(
                hidden, down_weight[0, low : low + piece], preferred_element_type=jnp.float32
            )
        low_half, high_half = out[:, :width_out], out[:, width_out:]
        mine = jnp.where(tp_index == 0, low_half, high_half)
        other = jnp.where(tp_index == 0, high_half, low_half).astype(jnp.bfloat16)
        swapped = lax.ppermute(other, "tp", [(0, 1), (1, 0)])
        core_summed = (mine + swapped.astype(jnp.float32)).astype(jnp.bfloat16)
        returned = lax.all_to_all(
            core_summed.reshape(ctx_count, C, width_out),
            "ctx",
            split_axis=0,
            concat_axis=0,
            tiled=True,
        ).astype(jnp.float32)
        summed = jnp.sum(returned.reshape(-1, ctx_sharing, C, width_out), axis=1)
        moe_mine = moe_mine + jnp.dot(
            combine_parts[:, :, e].reshape(row_count, -1),
            summed.reshape(-1, width_out),
            precision=highest,
        )
    return (mixed_in + moe_mine).astype(jnp.bfloat16)


def solution(mesh):
    return jax.shard_map(
        per_device,
        mesh=mesh,
        in_specs=(
            P(("groups", "ctx"), ("exp", "tp")),
            P(("groups", "ctx"), "exp"),
            P(("groups", "ctx"), "exp"),
            P(("groups", "ctx"), ("exp", "tp")),
            P(("exp", "tp")),
            P(("exp", "tp"), None),
            P(("groups", "ctx"), None),
            P("exp", "tp", "ctx"),
            P("tp", "ctx", "exp"),
        ),
        out_specs=P(("groups", "ctx"), ("exp", "tp")),
        check_vma=False,
    )
```

```python
import math

import jax
import jax.numpy as jnp
from jax import lax
from jax.sharding import PartitionSpec as P

HD = 128
QH = 24
KVH = 4
E = 8
C = 48
PIECES = 4


epsilon = 1e-05
highest = lax.Precision.HIGHEST
floor_score = -1e30


def per_device(
    query_rows,
    key_rows,
    value_rows,
    residual,
    norm_gain,
    router_weight,
    expert_ids,
    gate_weight,
    down_weight,
):
    ctx_count = lax.axis_size("ctx")
    exp_count = lax.axis_size("exp")
    tp_count = lax.axis_size("tp")
    tp_index = lax.axis_index("tp")
    row_count = query_rows.shape[0]
    kv_local = key_rows.shape[1] // HD
    query_local = query_rows.shape[1] // HD
    group_size = QH // KVH
    assert group_size % query_local == 0 and tp_count == 2
    owner = (tp_index * query_local) // group_size
    first_row = lax.axis_index("ctx") * row_count
    query_pos = first_row + jnp.arange(row_count, dtype=jnp.int32)
    query_heads = query_rows.reshape(row_count, query_local, HD)

    def own_head(rows):
        return lax.dynamic_slice_in_dim(rows, owner * HD, HD, axis=1)

    pair = jnp.concatenate([own_head(key_rows), own_head(value_rows)], axis=1)
    direct = ctx_count <= 4 and E % ctx_count == 0
    if direct:
        pieces_kv = [pair]
        for shift in range(1, ctx_count):
            later = [(j, j + shift) for j in range(ctx_count - shift)]
            pieces_kv.append(lax.ppermute(pair, "ctx", later))
        pair = jnp.concatenate(pieces_kv, axis=0)
        column = jnp.arange(pair.shape[0], dtype=jnp.int32)
        key_pos = first_row + column - 2 * (column // row_count) * row_count
        visible = (query_pos[:, None] >= key_pos[None, :]) & (key_pos >= 0)[None, :]
    else:
        pair = lax.all_gather(pair, "ctx", axis=0, tiled=True)
        visible = query_pos[:, None] >= jnp.arange(pair.shape[0], dtype=jnp.int32)[None, :]
    key_head, value_head = pair[:, :HD], pair[:, HD:]
    scores = jnp.einsum(
        "tqd,sd->qts", query_heads, key_head, preferred_element_type=jnp.float32
    ) * (1.0 / math.sqrt(HD))
    scores = jnp.where(visible[None], scores, floor_score)
    weights = jnp.exp(scores - jnp.max(scores, axis=-1, keepdims=True))
    run_total = jnp.sum(weights, axis=-1, keepdims=True)
    accumulated = jnp.einsum(
        "qts,sd->qtd",
        weights.astype(jnp.bfloat16),
        value_head,
        preferred_element_type=jnp.float32,
    )
    attended = jnp.transpose(accumulated / run_total, (1, 0, 2)).reshape(row_count, -1)
    mixed_in = residual.astype(jnp.float32) + attended
    scaled = mixed_in * norm_gain[None, :]
    square_sum = jnp.sum(mixed_in * mixed_in, axis=1)
    logit_part = jnp.dot(scaled, router_weight, precision=highest)
    ways = exp_count * tp_count
    if ways == 4:
        stats = jnp.concatenate([logit_part, square_sum[:, None]], axis=1).T
        for flip in (1, 2):
            stats = stats + lax.ppermute(stats, ("exp", "tp"), [(j, j ^ flip) for j in range(ways)])
        logit_part, square_sum = stats[:E].T, stats[E]
    else:
        square_sum, logit_part = lax.psum((square_sum, logit_part), ("exp", "tp"))
    inv_rms = lax.rsqrt(square_sum / (QH * HD) + epsilon)
    moe_half = (scaled * inv_rms[:, None]).astype(jnp.bfloat16)
    logits = logit_part * inv_rms[:, None]
    expert_range = jnp.arange(E, dtype=jnp.int32)
    chosen_hot = expert_ids[:, :, None] == expert_range[None, None, :]
    picked = jnp.sum(jnp.where(chosen_hot, logits[:, None, :], 0.0), axis=2)
    gate_pair = jnp.stack(
        [jax.nn.sigmoid(picked[:, 0] - picked[:, 1]), jax.nn.sigmoid(picked[:, 1] - picked[:, 0])],
        axis=1,
    )
    flat_ids = expert_ids.reshape(-1)
    flat_hot = (flat_ids[:, None] == expert_range[None, :]).astype(jnp.int32)
    slot_index = jnp.sum((jnp.cumsum(flat_hot, axis=0) - flat_hot) * flat_hot, axis=1)
    ctx_sharing = max(1, ctx_count // E)
    experts_held = max(1, E // ctx_count)
    if direct:
        away = (flat_ids // experts_held - lax.axis_index("ctx") + ctx_count) % ctx_count
        tile_index = (flat_ids % experts_held) * ctx_count + away
    else:
        tile_index = (flat_ids % experts_held) * (E // experts_held) + flat_ids // experts_held
    tile_row = (tile_index * C + slot_index).reshape(row_count, 2)
    tile_range = jnp.arange(E * C, dtype=jnp.int32)
    tile_hot = tile_row[:, :, None] == tile_range[None, None, :]
    combine_matrix = jnp.sum(jnp.where(tile_hot, gate_pair[:, :, None], 0.0), axis=1)
    dispatch_matrix = jnp.transpose(jnp.any(tile_hot, axis=1)).astype(jnp.bfloat16)
    send_tiles = jnp.dot(dispatch_matrix, moe_half, preferred_element_type=jnp.float32).astype(
        jnp.bfloat16
    )
    send_tiles = send_tiles.reshape(experts_held, E // experts_held, C, -1)

    def exchange(tiles, sign):
        if not direct:
            return lax.all_to_all(tiles, "ctx", split_axis=0, concat_axis=0, tiled=True)
        moved = [tiles[0]]
        for shift in range(1, ctx_count):
            turned = [(j, (j + sign * shift) % ctx_count) for j in range(ctx_count)]
            moved.append(lax.ppermute(tiles[shift], "ctx", turned))
        return jnp.stack(moved)

    hidden_width = gate_weight.shape[2] // experts_held
    pieces = max(1, min(PIECES, hidden_width // 512))
    piece = hidden_width // pieces
    halves = [
        exchange(jnp.repeat(send_tiles[e], ctx_sharing, axis=0), 1).reshape(ctx_count * C, -1)
        for e in range(experts_held)
    ]
    came = []
    sums = []
    for e in range(experts_held):
        half = halves[e]
        if came:
            half, came[0] = lax.optimization_barrier((half, came[0]))
        arrived = lax.all_gather(half, "tp", axis=1, tiled=True)
        for i in range(pieces):
            low = e * hidden_width + i * piece
            if len(came) >= 2:
                arrived, came[-2] = lax.optimization_barrier((arrived, came[-2]))
            part = jnp.dot(
                arrived,
                gate_weight[:, 0, low : low + piece],
                preferred_element_type=jnp.float32,
            ).astype(jnp.bfloat16)
            others = []
            for shift in range(1, exp_count):
                turned = [(j, (j + shift) % exp_count) for j in range(exp_count)]
                others.append(lax.ppermute(part, "exp", turned))
            came.append(others)
            sums.append(part)

    def total_of(k):
        return sum([p.astype(jnp.float32) for p in came[k]], sums[k].astype(jnp.float32))

    width_out = down_weight.shape[2] // tp_count
    moe_mine = 0.0
    combine_parts = combine_matrix.reshape(row_count, experts_held, -1)
    for e in range(experts_held):
        out = 0.0
        for i in range(pieces):
            low = e * hidden_width + i * piece
            hidden = jax.nn.silu(total_of(e * pieces + i)).astype(jnp.bfloat16)
            out = out + jnp.dot(
                hidden, down_weight[0, low : low + piece], preferred_element_type=jnp.float32
            )
        low_half, high_half = out[:, :width_out], out[:, width_out:]
        mine = jnp.where(tp_index == 0, low_half, high_half)
        other = jnp.where(tp_index == 0, high_half, low_half).astype(jnp.bfloat16)
        swapped = lax.ppermute(other, "tp", [(0, 1), (1, 0)])
        core_summed = (mine + swapped.astype(jnp.float32)).astype(jnp.bfloat16)
        returned = exchange(core_summed.reshape(ctx_count, C, width_out), -1).astype(jnp.float32)
        summed = jnp.sum(returned.reshape(-1, ctx_sharing, C, width_out), axis=1)
        moe_mine = moe_mine + jnp.dot(
            combine_parts[:, e],
            summed.reshape(-1, width_out),
            precision=highest,
        )
    return (mixed_in + moe_mine).astype(jnp.bfloat16)


def solution(mesh):
    return jax.shard_map(
        per_device,
        mesh=mesh,
        in_specs=(
            P(("groups", "ctx"), ("exp", "tp")),
            P(("groups", "ctx"), "exp"),
            P(("groups", "ctx"), "exp"),
            P(("groups", "ctx"), ("exp", "tp")),
            P(("exp", "tp")),
            P(("exp", "tp"), None),
            P(("groups", "ctx"), None),
            P("exp", "tp", "ctx"),
            P("tp", "ctx", "exp"),
        ),
        out_specs=P(("groups", "ctx"), ("exp", "tp")),
        check_vma=False,
    )
```

```python
import math

import jax
import jax.numpy as jnp
from jax import lax
from jax.experimental import pallas as pl
from jax.experimental.pallas import tpu as pltpu
from jax.sharding import PartitionSpec as P

HD = 128
QH = 24
KVH = 4
E = 8
C = 48
PIECES = 4


epsilon = 1e-05
highest = lax.Precision.HIGHEST
floor_score = -1e30


MESH = pl.DeviceIdType.MESH
WIDTH = 512
LAG = 3


def expert_kernel(
    n, held, pieces, tiles, gate, down, out,
    rows, gate_buf, down_buf, part, came, acc, swap_out, swap_in, back, landed,
    gate_sem, down_sem, go_send, go_recv, pass_send, pass_recv, x_send, x_recv,
    swap_send, swap_recv, back_send, back_recv,
):
    me, exp, tp = lax.axis_index("ctx"), lax.axis_index("exp"), lax.axis_index("tp")
    total = held * pieces
    count, half = rows.shape[2], rows.shape[3]

    def fetch_gate(k):
        columns = pl.ds(pl.multiple_of(k * WIDTH, WIDTH), WIDTH)
        return pltpu.make_async_copy(gate.at[:, columns], gate_buf.at[k % 2], gate_sem.at[k % 2])

    def fetch_down(k):
        lines = pl.ds(pl.multiple_of(k * WIDTH, WIDTH), WIDTH)
        return pltpu.make_async_copy(down.at[lines], down_buf.at[k % 2], down_sem.at[k % 2])

    def remote(src, dst, send, recv, where):
        return pltpu.make_async_remote_copy(
            src_ref=src, dst_ref=dst, send_sem=send, recv_sem=recv,
            device_id=where, device_id_type=MESH,
        )

    def go(e, shift):
        spot = pl.ds(shift * C, C)
        return remote(
            tiles.at[e, spot], rows.at[e, tp, spot], go_send.at[e, shift], go_recv.at[e, shift],
            {"ctx": lax.rem(me + shift, n)},
        )

    def hand_over(e):
        return remote(
            rows.at[e, tp], rows.at[e, tp], pass_send.at[e], pass_recv.at[e], {"tp": 1 - tp}
        )

    def cross(k):
        return remote(part.at[k], came.at[k], x_send.at[k], x_recv.at[k], {"exp": 1 - exp})

    def swap(e):
        return remote(swap_out.at[e], swap_in.at[e], swap_send.at[e], swap_recv.at[e], {"tp": 1 - tp})

    def give(e, shift):
        spot = pl.ds(shift * C, C)
        return remote(
            back.at[e, spot], landed.at[e, spot], back_send.at[e, shift], back_recv.at[e, shift],
            {"ctx": lax.rem(me + n - shift, n)},
        )

    fetch_gate(0).start()
    fetch_down(0).start()
    barrier = pltpu.get_barrier_semaphore()
    for shift in range(1, n):
        pl.semaphore_signal(
            barrier, inc=1, device_id={"ctx": lax.rem(me + shift, n)}, device_id_type=MESH
        )
    pl.semaphore_signal(barrier, inc=1, device_id={"exp": 1 - exp}, device_id_type=MESH)
    pl.semaphore_signal(barrier, inc=1, device_id={"tp": 1 - tp}, device_id_type=MESH)
    pl.semaphore_wait(barrier, n + 1)
    for e in range(held):
        for shift in range(1, n):
            go(e, shift).start()
    for e in range(held):
        rows[e, tp, :C] = tiles[e, :C]

    def step(k, carry):
        @pl.when(k < total)
        def _():
            e = k // pieces

            @pl.when(k % pieces == 0)
            def _():
                for shift in range(1, n):
                    go(e, shift).wait_recv()
                hand_over(e).start()
                hand_over(e).wait_recv()

            @pl.when(k + 1 < total)
            def _():
                fetch_gate(k + 1).start()

            fetch_gate(k).wait()
            product = jnp.dot(
                rows[e, 0], gate_buf[k % 2, :half], preferred_element_type=jnp.float32
            ) + jnp.dot(rows[e, 1], gate_buf[k % 2, half:], preferred_element_type=jnp.float32)
            part[k] = product.astype(jnp.bfloat16)
            cross(k).start()

        @pl.when(k >= LAG)
        def _():
            j = k - LAG
            e = j // pieces

            @pl.when(j + 1 < total)
            def _():
                fetch_down(j + 1).start()

            cross(j).wait_recv()
            pre_act = part[j].astype(jnp.float32) + came[j].astype(jnp.float32)
            hidden = jax.nn.silu(pre_act).astype(jnp.bfloat16)
            fetch_down(j).wait()
            product = jnp.dot(hidden, down_buf[j % 2], preferred_element_type=jnp.float32)

            @pl.when(j % pieces == 0)
            def _():
                acc[...] = product

            @pl.when(j % pieces != 0)
            def _():
                acc[...] += product

            @pl.when(j % pieces == pieces - 1)
            def _():
                far = pl.ds(pl.multiple_of((1 - tp) * half, 128), half)
                near = pl.ds(pl.multiple_of(tp * half, 128), half)
                swap_out[e] = acc[:, far].astype(jnp.bfloat16)
                swap(e).start()
                swap(e).wait_recv()
                back[e] = (acc[:, near] + swap_in[e].astype(jnp.float32)).astype(jnp.bfloat16)
                for shift in range(1, n):
                    give(e, shift).start()

        return carry

    lax.fori_loop(0, total + LAG, step, 0)
    for e in range(held):
        out[e, :C] = back[e, :C]
        for shift in range(1, n):
            give(e, shift).wait_recv()
            out[e, shift * C : (shift + 1) * C] = landed[e, shift * C : (shift + 1) * C]

    def drain(k, carry):
        cross(k).wait_send()
        return carry

    lax.fori_loop(0, total, drain, 0)
    for e in range(held):
        hand_over(e).wait_send()
        swap(e).wait_send()
        for shift in range(1, n):
            go(e, shift).wait_send()
            give(e, shift).wait_send()


def run_experts(tiles, gate, down, n, held):
    depth, units = gate.shape
    pieces = units // held // WIDTH
    total = held * pieces
    count, half = tiles.shape[1], tiles.shape[2]
    wide = down.shape[1]
    dma = pltpu.SemaphoreType.DMA
    return pl.pallas_call(
        lambda *refs: expert_kernel(n, held, pieces, *refs),
        out_shape=jax.ShapeDtypeStruct((held, count, wide // 2), jnp.bfloat16),
        in_specs=[
            pl.BlockSpec(memory_space=pltpu.VMEM),
            pl.BlockSpec(memory_space=pl.ANY),
            pl.BlockSpec(memory_space=pl.ANY),
        ],
        out_specs=pl.BlockSpec(memory_space=pltpu.VMEM),
        scratch_shapes=[
            pltpu.VMEM((held, 2, count, half), jnp.bfloat16),
            pltpu.VMEM((2, depth, WIDTH), jnp.bfloat16),
            pltpu.VMEM((2, WIDTH, wide), jnp.bfloat16),
            pltpu.VMEM((total, count, WIDTH), jnp.bfloat16),
            pltpu.VMEM((total, count, WIDTH), jnp.bfloat16),
            pltpu.VMEM((count, wide), jnp.float32),
            pltpu.VMEM((held, count, wide // 2), jnp.bfloat16),
            pltpu.VMEM((held, count, wide // 2), jnp.bfloat16),
            pltpu.VMEM((held, count, wide // 2), jnp.bfloat16),
            pltpu.VMEM((held, count, wide // 2), jnp.bfloat16),
            dma((2,)), dma((2,)),
            dma((held, n)), dma((held, n)),
            dma((held,)), dma((held,)),
            dma((total,)), dma((total,)),
            dma((held,)), dma((held,)),
            dma((held, n)), dma((held, n)),
        ],
        compiler_params=pltpu.CompilerParams(
            collective_id=0, has_side_effects=True, vmem_limit_bytes=48 * 2**20
        ),
        cost_estimate=pl.CostEstimate(
            flops=4 * held * count * depth * units // held, bytes_accessed=4 * depth * units,
            transcendentals=0,
        ),
    )(tiles, gate, down)


def per_device(
    query_rows,
    key_rows,
    value_rows,
    residual,
    norm_gain,
    router_weight,
    expert_ids,
    gate_weight,
    down_weight,
):
    ctx_count = lax.axis_size("ctx")
    exp_count = lax.axis_size("exp")
    tp_count = lax.axis_size("tp")
    tp_index = lax.axis_index("tp")
    row_count = query_rows.shape[0]
    kv_local = key_rows.shape[1] // HD
    query_local = query_rows.shape[1] // HD
    group_size = QH // KVH
    assert group_size % query_local == 0 and tp_count == 2
    owner = (tp_index * query_local) // group_size
    first_row = lax.axis_index("ctx") * row_count
    query_pos = first_row + jnp.arange(row_count, dtype=jnp.int32)
    query_heads = query_rows.reshape(row_count, query_local, HD)

    def own_head(rows):
        return lax.dynamic_slice_in_dim(rows, owner * HD, HD, axis=1)

    pair = jnp.concatenate([own_head(key_rows), own_head(value_rows)], axis=1)
    direct = ctx_count <= 4 and E % ctx_count == 0
    if direct:
        pieces_kv = [pair]
        for shift in range(1, ctx_count):
            later = [(j, j + shift) for j in range(ctx_count - shift)]
            pieces_kv.append(lax.ppermute(pair, "ctx", later))
        pair = jnp.concatenate(pieces_kv, axis=0)
        column = jnp.arange(pair.shape[0], dtype=jnp.int32)
        key_pos = first_row + column - 2 * (column // row_count) * row_count
        visible = (query_pos[:, None] >= key_pos[None, :]) & (key_pos >= 0)[None, :]
    else:
        pair = lax.all_gather(pair, "ctx", axis=0, tiled=True)
        visible = query_pos[:, None] >= jnp.arange(pair.shape[0], dtype=jnp.int32)[None, :]
    key_head, value_head = pair[:, :HD], pair[:, HD:]
    scores = jnp.einsum(
        "tqd,sd->qts", query_heads, key_head, preferred_element_type=jnp.float32
    ) * (1.0 / math.sqrt(HD))
    scores = jnp.where(visible[None], scores, floor_score)
    weights = jnp.exp(scores - jnp.max(scores, axis=-1, keepdims=True))
    run_total = jnp.sum(weights, axis=-1, keepdims=True)
    accumulated = jnp.einsum(
        "qts,sd->qtd",
        weights.astype(jnp.bfloat16),
        value_head,
        preferred_element_type=jnp.float32,
    )
    attended = jnp.transpose(accumulated / run_total, (1, 0, 2)).reshape(row_count, -1)
    mixed_in = residual.astype(jnp.float32) + attended
    scaled = mixed_in * norm_gain[None, :]
    square_sum = jnp.sum(mixed_in * mixed_in, axis=1)
    logit_part = jnp.dot(scaled, router_weight, precision=highest)
    ways = exp_count * tp_count
    if ways == 4:
        stats = jnp.concatenate([logit_part, square_sum[:, None]], axis=1).T
        for flip in (1, 2):
            stats = stats + lax.ppermute(stats, ("exp", "tp"), [(j, j ^ flip) for j in range(ways)])
        logit_part, square_sum = stats[:E].T, stats[E]
    else:
        square_sum, logit_part = lax.psum((square_sum, logit_part), ("exp", "tp"))
    inv_rms = lax.rsqrt(square_sum / (QH * HD) + epsilon)
    moe_half = (scaled * inv_rms[:, None]).astype(jnp.bfloat16)
    logits = logit_part * inv_rms[:, None]
    expert_range = jnp.arange(E, dtype=jnp.int32)
    chosen_hot = expert_ids[:, :, None] == expert_range[None, None, :]
    picked = jnp.sum(jnp.where(chosen_hot, logits[:, None, :], 0.0), axis=2)
    gate_pair = jnp.stack(
        [jax.nn.sigmoid(picked[:, 0] - picked[:, 1]), jax.nn.sigmoid(picked[:, 1] - picked[:, 0])],
        axis=1,
    )
    flat_ids = expert_ids.reshape(-1)
    flat_hot = (flat_ids[:, None] == expert_range[None, :]).astype(jnp.int32)
    slot_index = jnp.sum((jnp.cumsum(flat_hot, axis=0) - flat_hot) * flat_hot, axis=1)
    ctx_sharing = max(1, ctx_count // E)
    experts_held = max(1, E // ctx_count)
    if direct:
        away = (flat_ids // experts_held - lax.axis_index("ctx") + ctx_count) % ctx_count
        tile_index = (flat_ids % experts_held) * ctx_count + away
    else:
        tile_index = (flat_ids % experts_held) * (E // experts_held) + flat_ids // experts_held
    tile_row = (tile_index * C + slot_index).reshape(row_count, 2)
    tile_range = jnp.arange(E * C, dtype=jnp.int32)
    tile_hot = tile_row[:, :, None] == tile_range[None, None, :]
    combine_matrix = jnp.sum(jnp.where(tile_hot, gate_pair[:, :, None], 0.0), axis=1)
    dispatch_matrix = jnp.transpose(jnp.any(tile_hot, axis=1)).astype(jnp.bfloat16)
    send_tiles = jnp.dot(dispatch_matrix, moe_half, preferred_element_type=jnp.float32).astype(
        jnp.bfloat16
    )
    send_tiles = send_tiles.reshape(experts_held, E // experts_held, C, -1)

    if direct and exp_count == 2 and gate_weight.shape[2] // experts_held % WIDTH == 0:
        returned = run_experts(
            send_tiles.reshape(experts_held, ctx_count * C, -1),
            gate_weight.reshape(gate_weight.shape[0], -1),
            down_weight.reshape(-1, down_weight.shape[2]),
            ctx_count,
            experts_held,
        )
        moe_mine = jnp.dot(
            combine_matrix,
            returned.reshape(E * C, -1).astype(jnp.float32),
            precision=highest,
        )
        return (mixed_in + moe_mine).astype(jnp.bfloat16)

    def exchange(tiles, sign):
        if not direct:
            return lax.all_to_all(tiles, "ctx", split_axis=0, concat_axis=0, tiled=True)
        moved = [tiles[0]]
        for shift in range(1, ctx_count):
            turned = [(j, (j + sign * shift) % ctx_count) for j in range(ctx_count)]
            moved.append(lax.ppermute(tiles[shift], "ctx", turned))
        return jnp.stack(moved)

    hidden_width = gate_weight.shape[2] // experts_held
    pieces = max(1, min(PIECES, hidden_width // 512))
    piece = hidden_width // pieces
    halves = [
        exchange(jnp.repeat(send_tiles[e], ctx_sharing, axis=0), 1).reshape(ctx_count * C, -1)
        for e in range(experts_held)
    ]
    came = []
    sums = []
    for e in range(experts_held):
        half = halves[e]
        if came:
            half, came[0] = lax.optimization_barrier((half, came[0]))
        arrived = lax.all_gather(half, "tp", axis=1, tiled=True)
        for i in range(pieces):
            low = e * hidden_width + i * piece
            if len(came) >= 2:
                arrived, came[-2] = lax.optimization_barrier((arrived, came[-2]))
            part = jnp.dot(
                arrived,
                gate_weight[:, 0, low : low + piece],
                preferred_element_type=jnp.float32,
            ).astype(jnp.bfloat16)
            others = []
            for shift in range(1, exp_count):
                turned = [(j, (j + shift) % exp_count) for j in range(exp_count)]
                others.append(lax.ppermute(part, "exp", turned))
            came.append(others)
            sums.append(part)

    def total_of(k):
        return sum([p.astype(jnp.float32) for p in came[k]], sums[k].astype(jnp.float32))

    width_out = down_weight.shape[2] // tp_count
    moe_mine = 0.0
    combine_parts = combine_matrix.reshape(row_count, experts_held, -1)
    for e in range(experts_held):
        out = 0.0
        for i in range(pieces):
            low = e * hidden_width + i * piece
            hidden = jax.nn.silu(total_of(e * pieces + i)).astype(jnp.bfloat16)
            out = out + jnp.dot(
                hidden, down_weight[0, low : low + piece], preferred_element_type=jnp.float32
            )
        low_half, high_half = out[:, :width_out], out[:, width_out:]
        mine = jnp.where(tp_index == 0, low_half, high_half)
        other = jnp.where(tp_index == 0, high_half, low_half).astype(jnp.bfloat16)
        swapped = lax.ppermute(other, "tp", [(0, 1), (1, 0)])
        core_summed = (mine + swapped.astype(jnp.float32)).astype(jnp.bfloat16)
        returned = exchange(core_summed.reshape(ctx_count, C, width_out), -1).astype(jnp.float32)
        summed = jnp.sum(returned.reshape(-1, ctx_sharing, C, width_out), axis=1)
        moe_mine = moe_mine + jnp.dot(
            combine_parts[:, e],
            summed.reshape(-1, width_out),
            precision=highest,
        )
    return (mixed_in + moe_mine).astype(jnp.bfloat16)


def solution(mesh):
    return jax.shard_map(
        per_device,
        mesh=mesh,
        in_specs=(
            P(("groups", "ctx"), ("exp", "tp")),
            P(("groups", "ctx"), "exp"),
            P(("groups", "ctx"), "exp"),
            P(("groups", "ctx"), ("exp", "tp")),
            P(("exp", "tp")),
            P(("exp", "tp"), None),
            P(("groups", "ctx"), None),
            P("exp", "tp", "ctx"),
            P("tp", "ctx", "exp"),
        ),
        out_specs=P(("groups", "ctx"), ("exp", "tp")),
        check_vma=False,
    )
```

```python
import math

import jax
import jax.numpy as jnp
from jax import lax
from jax.experimental import pallas as pl
from jax.experimental.pallas import tpu as pltpu
from jax.sharding import PartitionSpec as P

HD = 128
QH = 24
KVH = 4
E = 8
C = 48
PIECES = 4


epsilon = 1e-05
highest = lax.Precision.HIGHEST
floor_score = -1e30


MESH = pl.DeviceIdType.MESH
WIDTH = 1024
LAG = 3


def expert_kernel(
    n, held, pieces, tiles, gate, down, out,
    rows, gate_buf, down_buf, part, came, acc, swap_out, swap_in, back, landed,
    gate_sem, down_sem, go_send, go_recv, pass_send, pass_recv, x_send, x_recv,
    swap_send, swap_recv, back_send, back_recv,
):
    me, exp, tp = lax.axis_index("ctx"), lax.axis_index("exp"), lax.axis_index("tp")
    units = 2 * held
    per = n // 2
    total = units * pieces
    half = rows.shape[3]

    def shift_of(u, p):
        spot = (u % 2) * per + p
        return (spot + per) % n if u // 2 == held - 1 else spot

    every = [(u, p) for u in range(units) for p in range(per)]
    away = [(u, p) for u, p in every if shift_of(u, p)]
    here = [(u, p) for u, p in every if not shift_of(u, p)]

    def block_of(k):
        place = (k // pieces // 2) * pieces + k % pieces
        return pl.ds(pl.multiple_of(place * WIDTH, WIDTH), WIDTH)

    def fetch_gate(k):
        return pltpu.make_async_copy(gate.at[:, block_of(k)], gate_buf.at[k % 2], gate_sem.at[k % 2])

    def fetch_down(k):
        return pltpu.make_async_copy(down.at[block_of(k)], down_buf.at[k % 2], down_sem.at[k % 2])

    def remote(src, dst, send, recv, where):
        return pltpu.make_async_remote_copy(
            src_ref=src, dst_ref=dst, send_sem=send, recv_sem=recv,
            device_id=where, device_id_type=MESH,
        )

    def go(u, p):
        spot = pl.ds(p * C, C)
        return remote(
            tiles.at[u, spot], rows.at[u, tp, spot], go_send.at[u, p], go_recv.at[u, p],
            {"ctx": lax.rem(me + shift_of(u, p), n)},
        )

    def hand_over(e):
        return remote(
            rows.at[e, tp], rows.at[e, tp], pass_send.at[e], pass_recv.at[e], {"tp": 1 - tp}
        )

    def cross(k):
        return remote(part.at[k], came.at[k], x_send.at[k], x_recv.at[k], {"exp": 1 - exp})

    def swap(e):
        return remote(swap_out.at[e], swap_in.at[e], swap_send.at[e], swap_recv.at[e], {"tp": 1 - tp})

    def give(u, p):
        spot = pl.ds(p * C, C)
        return remote(
            back.at[u, spot], landed.at[u, spot], back_send.at[u, p], back_recv.at[u, p],
            {"ctx": lax.rem(me + n - shift_of(u, p), n)},
        )

    fetch_gate(0).start()
    fetch_down(0).start()
    barrier = pltpu.get_barrier_semaphore()
    for shift in range(1, n):
        pl.semaphore_signal(
            barrier, inc=1, device_id={"ctx": lax.rem(me + shift, n)}, device_id_type=MESH
        )
    pl.semaphore_signal(barrier, inc=1, device_id={"exp": 1 - exp}, device_id_type=MESH)
    pl.semaphore_signal(barrier, inc=1, device_id={"tp": 1 - tp}, device_id_type=MESH)
    pl.semaphore_wait(barrier, n + 1)
    for u, p in away:
        if u == 0:
            go(u, p).start()
    for u, p in here:
        rows[u, tp, p * C : (p + 1) * C] = tiles[u, p * C : (p + 1) * C]

    def receive(u):
        for v, p in away:
            if v == u:
                go(v, p).wait_recv()
        hand_over(u).start()
        for v, p in away:
            if v == u + 1:
                go(v, p).start()
        hand_over(u).wait_recv()

    def finish(u):
        far = pl.ds(pl.multiple_of((1 - tp) * half, 128), half)
        near = pl.ds(pl.multiple_of(tp * half, 128), half)
        swap_out[u] = acc[:, far].astype(jnp.bfloat16)
        swap(u).start()
        swap(u).wait_recv()
        back[u] = (acc[:, near] + swap_in[u].astype(jnp.float32)).astype(jnp.bfloat16)
        for v, p in away:
            if v == u:
                give(v, p).start()

    def step(k, carry):
        @pl.when(k < total)
        def _():
            e = k // pieces
            for u in range(units):
                pl.when(k == u * pieces)(lambda u=u: receive(u))

            @pl.when(k + 1 < total)
            def _():
                fetch_gate(k + 1).start()

            fetch_gate(k).wait()
            product = jnp.dot(
                rows[e, 0], gate_buf[k % 2, :half], preferred_element_type=jnp.float32
            ) + jnp.dot(rows[e, 1], gate_buf[k % 2, half:], preferred_element_type=jnp.float32)
            part[k] = product.astype(jnp.bfloat16)
            cross(k).start()

        @pl.when(k >= LAG)
        def _():
            j = k - LAG
            e = j // pieces

            @pl.when(j + 1 < total)
            def _():
                fetch_down(j + 1).start()

            cross(j).wait_recv()
            pre_act = part[j].astype(jnp.float32) + came[j].astype(jnp.float32)
            hidden = jax.nn.silu(pre_act).astype(jnp.bfloat16)
            fetch_down(j).wait()
            product = jnp.dot(hidden, down_buf[j % 2], preferred_element_type=jnp.float32)

            @pl.when(j % pieces == 0)
            def _():
                acc[...] = product

            @pl.when(j % pieces != 0)
            def _():
                acc[...] += product

            for u in range(units):
                pl.when(j == (u + 1) * pieces - 1)(lambda u=u: finish(u))

        return carry

    lax.fori_loop(0, total + LAG, step, 0)
    for u, p in here:
        out[u, p * C : (p + 1) * C] = back[u, p * C : (p + 1) * C]
    for u, p in away:
        give(u, p).wait_recv()
        out[u, p * C : (p + 1) * C] = landed[u, p * C : (p + 1) * C]

    def drain(k, carry):
        cross(k).wait_send()
        return carry

    lax.fori_loop(0, total, drain, 0)
    for u in range(units):
        hand_over(u).wait_send()
        swap(u).wait_send()
    for u, p in away:
        go(u, p).wait_send()
        give(u, p).wait_send()


def run_experts(tiles, gate, down, n, held):
    depth, units = gate.shape
    pieces = units // held // WIDTH
    parts = 2 * held
    total = parts * pieces
    count, half = tiles.shape[1], tiles.shape[2]
    wide = down.shape[1]
    dma = pltpu.SemaphoreType.DMA
    return pl.pallas_call(
        lambda *refs: expert_kernel(n, held, pieces, *refs),
        out_shape=jax.ShapeDtypeStruct((parts, count, wide // 2), jnp.bfloat16),
        in_specs=[
            pl.BlockSpec(memory_space=pltpu.VMEM),
            pl.BlockSpec(memory_space=pl.ANY),
            pl.BlockSpec(memory_space=pl.ANY),
        ],
        out_specs=pl.BlockSpec(memory_space=pltpu.VMEM),
        scratch_shapes=[
            pltpu.VMEM((parts, 2, count, half), jnp.bfloat16),
            pltpu.VMEM((2, depth, WIDTH), jnp.bfloat16),
            pltpu.VMEM((2, WIDTH, wide), jnp.bfloat16),
            pltpu.VMEM((total, count, WIDTH), jnp.bfloat16),
            pltpu.VMEM((total, count, WIDTH), jnp.bfloat16),
            pltpu.VMEM((count, wide), jnp.float32),
            pltpu.VMEM((parts, count, wide // 2), jnp.bfloat16),
            pltpu.VMEM((parts, count, wide // 2), jnp.bfloat16),
            pltpu.VMEM((parts, count, wide // 2), jnp.bfloat16),
            pltpu.VMEM((parts, count, wide // 2), jnp.bfloat16),
            dma((2,)), dma((2,)),
            dma((parts, n // 2)), dma((parts, n // 2)),
            dma((parts,)), dma((parts,)),
            dma((total,)), dma((total,)),
            dma((parts,)), dma((parts,)),
            dma((parts, n // 2)), dma((parts, n // 2)),
        ],
        compiler_params=pltpu.CompilerParams(
            collective_id=0, has_side_effects=True, vmem_limit_bytes=48 * 2**20
        ),
        cost_estimate=pl.CostEstimate(
            flops=8 * held * count * depth * units // held, bytes_accessed=8 * depth * units,
            transcendentals=0,
        ),
    )(tiles, gate, down)


def per_device(
    query_rows,
    key_rows,
    value_rows,
    residual,
    norm_gain,
    router_weight,
    expert_ids,
    gate_weight,
    down_weight,
):
    ctx_count = lax.axis_size("ctx")
    exp_count = lax.axis_size("exp")
    tp_count = lax.axis_size("tp")
    tp_index = lax.axis_index("tp")
    row_count = query_rows.shape[0]
    kv_local = key_rows.shape[1] // HD
    query_local = query_rows.shape[1] // HD
    group_size = QH // KVH
    assert group_size % query_local == 0 and tp_count == 2
    owner = (tp_index * query_local) // group_size
    first_row = lax.axis_index("ctx") * row_count
    query_pos = first_row + jnp.arange(row_count, dtype=jnp.int32)
    query_heads = query_rows.reshape(row_count, query_local, HD)

    def own_head(rows):
        return lax.dynamic_slice_in_dim(rows, owner * HD, HD, axis=1)

    pair = jnp.concatenate([own_head(key_rows), own_head(value_rows)], axis=1)
    direct = ctx_count <= 4 and E % ctx_count == 0
    if direct:
        pieces_kv = [pair]
        for shift in range(1, ctx_count):
            later = [(j, j + shift) for j in range(ctx_count - shift)]
            pieces_kv.append(lax.ppermute(pair, "ctx", later))
        pair = jnp.concatenate(pieces_kv, axis=0)
        column = jnp.arange(pair.shape[0], dtype=jnp.int32)
        key_pos = first_row + column - 2 * (column // row_count) * row_count
        visible = (query_pos[:, None] >= key_pos[None, :]) & (key_pos >= 0)[None, :]
    else:
        pair = lax.all_gather(pair, "ctx", axis=0, tiled=True)
        visible = query_pos[:, None] >= jnp.arange(pair.shape[0], dtype=jnp.int32)[None, :]
    key_head, value_head = pair[:, :HD], pair[:, HD:]
    scores = jnp.einsum(
        "tqd,sd->qts", query_heads, key_head, preferred_element_type=jnp.float32
    ) * (1.0 / math.sqrt(HD))
    scores = jnp.where(visible[None], scores, floor_score)
    weights = jnp.exp(scores - jnp.max(scores, axis=-1, keepdims=True))
    run_total = jnp.sum(weights, axis=-1, keepdims=True)
    accumulated = jnp.einsum(
        "qts,sd->qtd",
        weights.astype(jnp.bfloat16),
        value_head,
        preferred_element_type=jnp.float32,
    )
    attended = jnp.transpose(accumulated / run_total, (1, 0, 2)).reshape(row_count, -1)
    mixed_in = residual.astype(jnp.float32) + attended
    scaled = mixed_in * norm_gain[None, :]
    square_sum = jnp.sum(mixed_in * mixed_in, axis=1)
    logit_part = jnp.dot(scaled, router_weight, precision=highest)
    ways = exp_count * tp_count
    if ways == 4:
        stats = jnp.concatenate([logit_part, square_sum[:, None]], axis=1).T
        for flip in (1, 2):
            stats = stats + lax.ppermute(stats, ("exp", "tp"), [(j, j ^ flip) for j in range(ways)])
        logit_part, square_sum = stats[:E].T, stats[E]
    else:
        square_sum, logit_part = lax.psum((square_sum, logit_part), ("exp", "tp"))
    inv_rms = lax.rsqrt(square_sum / (QH * HD) + epsilon)
    moe_half = (scaled * inv_rms[:, None]).astype(jnp.bfloat16)
    logits = logit_part * inv_rms[:, None]
    expert_range = jnp.arange(E, dtype=jnp.int32)
    chosen_hot = expert_ids[:, :, None] == expert_range[None, None, :]
    picked = jnp.sum(jnp.where(chosen_hot, logits[:, None, :], 0.0), axis=2)
    gate_pair = jnp.stack(
        [jax.nn.sigmoid(picked[:, 0] - picked[:, 1]), jax.nn.sigmoid(picked[:, 1] - picked[:, 0])],
        axis=1,
    )
    flat_ids = expert_ids.reshape(-1)
    flat_hot = (flat_ids[:, None] == expert_range[None, :]).astype(jnp.int32)
    slot_index = jnp.sum((jnp.cumsum(flat_hot, axis=0) - flat_hot) * flat_hot, axis=1)
    ctx_sharing = max(1, ctx_count // E)
    experts_held = max(1, E // ctx_count)
    kernel_path = (
        direct
        and exp_count == 2
        and ctx_count % 2 == 0
        and gate_weight.shape[2] // experts_held % WIDTH == 0
    )
    if direct:
        away = (flat_ids // experts_held - lax.axis_index("ctx") + ctx_count) % ctx_count
        local = flat_ids % experts_held
        if kernel_path:
            away = (away + (local == experts_held - 1) * (ctx_count // 2)) % ctx_count
        tile_index = local * ctx_count + away
    else:
        tile_index = (flat_ids % experts_held) * (E // experts_held) + flat_ids // experts_held
    tile_row = (tile_index * C + slot_index).reshape(row_count, 2)
    tile_range = jnp.arange(E * C, dtype=jnp.int32)
    tile_hot = tile_row[:, :, None] == tile_range[None, None, :]
    combine_matrix = jnp.sum(jnp.where(tile_hot, gate_pair[:, :, None], 0.0), axis=1)
    dispatch_matrix = jnp.transpose(jnp.any(tile_hot, axis=1)).astype(jnp.bfloat16)
    send_tiles = jnp.dot(dispatch_matrix, moe_half, preferred_element_type=jnp.float32).astype(
        jnp.bfloat16
    )
    send_tiles = send_tiles.reshape(experts_held, E // experts_held, C, -1)

    if kernel_path:
        returned = run_experts(
            send_tiles.reshape(2 * experts_held, ctx_count // 2 * C, -1),
            gate_weight.reshape(gate_weight.shape[0], -1),
            down_weight.reshape(-1, down_weight.shape[2]),
            ctx_count,
            experts_held,
        )
        moe_mine = jnp.dot(
            combine_matrix,
            returned.reshape(E * C, -1).astype(jnp.float32),
            precision=highest,
        )
        return (mixed_in + moe_mine).astype(jnp.bfloat16)

    def exchange(tiles, sign):
        if not direct:
            return lax.all_to_all(tiles, "ctx", split_axis=0, concat_axis=0, tiled=True)
        moved = [tiles[0]]
        for shift in range(1, ctx_count):
            turned = [(j, (j + sign * shift) % ctx_count) for j in range(ctx_count)]
            moved.append(lax.ppermute(tiles[shift], "ctx", turned))
        return jnp.stack(moved)

    hidden_width = gate_weight.shape[2] // experts_held
    pieces = max(1, min(PIECES, hidden_width // 512))
    piece = hidden_width // pieces
    halves = [
        exchange(jnp.repeat(send_tiles[e], ctx_sharing, axis=0), 1).reshape(ctx_count * C, -1)
        for e in range(experts_held)
    ]
    came = []
    sums = []
    for e in range(experts_held):
        half = halves[e]
        if came:
            half, came[0] = lax.optimization_barrier((half, came[0]))
        arrived = lax.all_gather(half, "tp", axis=1, tiled=True)
        for i in range(pieces):
            low = e * hidden_width + i * piece
            if len(came) >= 2:
                arrived, came[-2] = lax.optimization_barrier((arrived, came[-2]))
            part = jnp.dot(
                arrived,
                gate_weight[:, 0, low : low + piece],
                preferred_element_type=jnp.float32,
            ).astype(jnp.bfloat16)
            others = []
            for shift in range(1, exp_count):
                turned = [(j, (j + shift) % exp_count) for j in range(exp_count)]
                others.append(lax.ppermute(part, "exp", turned))
            came.append(others)
            sums.append(part)

    def total_of(k):
        return sum([p.astype(jnp.float32) for p in came[k]], sums[k].astype(jnp.float32))

    width_out = down_weight.shape[2] // tp_count
    moe_mine = 0.0
    combine_parts = combine_matrix.reshape(row_count, experts_held, -1)
    for e in range(experts_held):
        out = 0.0
        for i in range(pieces):
            low = e * hidden_width + i * piece
            hidden = jax.nn.silu(total_of(e * pieces + i)).astype(jnp.bfloat16)
            out = out + jnp.dot(
                hidden, down_weight[0, low : low + piece], preferred_element_type=jnp.float32
            )
        low_half, high_half = out[:, :width_out], out[:, width_out:]
        mine = jnp.where(tp_index == 0, low_half, high_half)
        other = jnp.where(tp_index == 0, high_half, low_half).astype(jnp.bfloat16)
        swapped = lax.ppermute(other, "tp", [(0, 1), (1, 0)])
        core_summed = (mine + swapped.astype(jnp.float32)).astype(jnp.bfloat16)
        returned = exchange(core_summed.reshape(ctx_count, C, width_out), -1).astype(jnp.float32)
        summed = jnp.sum(returned.reshape(-1, ctx_sharing, C, width_out), axis=1)
        moe_mine = moe_mine + jnp.dot(
            combine_parts[:, e],
            summed.reshape(-1, width_out),
            precision=highest,
        )
    return (mixed_in + moe_mine).astype(jnp.bfloat16)


def solution(mesh):
    return jax.shard_map(
        per_device,
        mesh=mesh,
        in_specs=(
            P(("groups", "ctx"), ("exp", "tp")),
            P(("groups", "ctx"), "exp"),
            P(("groups", "ctx"), "exp"),
            P(("groups", "ctx"), ("exp", "tp")),
            P(("exp", "tp")),
            P(("exp", "tp"), None),
            P(("groups", "ctx"), None),
            P("exp", "tp", "ctx"),
            P("tp", "ctx", "exp"),
        ),
        out_specs=P(("groups", "ctx"), ("exp", "tp")),
        check_vma=False,
    )
```

```python
import math

import jax
import jax.numpy as jnp
from jax import lax
from jax.experimental import pallas as pl
from jax.experimental.pallas import tpu as pltpu
from jax.sharding import PartitionSpec as P

HD = 128
QH = 24
KVH = 4
E = 8
C = 48
PIECES = 4


epsilon = 1e-05
highest = lax.Precision.HIGHEST
floor_score = -1e30


MESH = pl.DeviceIdType.MESH
WIDTH = 1024
LAG = 3


def expert_kernel(
    n, held, pieces, tiles, gate, down, out,
    rows, gate_buf, down_buf, part, came, acc, swap_out, swap_in, back, landed,
    gate_sem, down_sem, go_send, go_recv, pass_send, pass_recv, x_send, x_recv,
    swap_send, swap_recv, back_send, back_recv,
):
    me, exp, tp = lax.axis_index("ctx"), lax.axis_index("exp"), lax.axis_index("tp")
    units = 2 * held
    per = n // 2
    total = units * pieces
    half = rows.shape[3]

    def shift_of(u, p):
        spot = (u % 2) * per + p
        return (spot + per) % n if u // 2 == held - 1 else spot

    every = [(u, p) for u in range(units) for p in range(per)]
    away = [(u, p) for u, p in every if shift_of(u, p)]
    here = [(u, p) for u, p in every if not shift_of(u, p)]

    def block_of(k):
        place = (k // pieces // 2) * pieces + k % pieces
        return pl.ds(pl.multiple_of(place * WIDTH, WIDTH), WIDTH)

    def fetch_gate(k):
        return pltpu.make_async_copy(gate.at[:, block_of(k)], gate_buf.at[k % 2], gate_sem.at[k % 2])

    def fetch_down(k):
        return pltpu.make_async_copy(down.at[block_of(k)], down_buf.at[k % 2], down_sem.at[k % 2])

    def remote(src, dst, send, recv, where):
        return pltpu.make_async_remote_copy(
            src_ref=src, dst_ref=dst, send_sem=send, recv_sem=recv,
            device_id=where, device_id_type=MESH,
        )

    def go(u, p):
        spot = pl.ds(p * C, C)
        return remote(
            tiles.at[u, spot], rows.at[u, tp, spot], go_send.at[u, p], go_recv.at[u, p],
            {"ctx": lax.rem(me + shift_of(u, p), n)},
        )

    def hand_over(e):
        return remote(
            rows.at[e, tp], rows.at[e, tp], pass_send.at[e], pass_recv.at[e], {"tp": 1 - tp}
        )

    def cross(k):
        return remote(part.at[k], came.at[k], x_send.at[k], x_recv.at[k], {"exp": 1 - exp})

    def swap(e):
        return remote(swap_out.at[e], swap_in.at[e], swap_send.at[e], swap_recv.at[e], {"tp": 1 - tp})

    def give(u, p):
        spot = pl.ds(p * C, C)
        return remote(
            back.at[u, spot], landed.at[u, spot], back_send.at[u, p], back_recv.at[u, p],
            {"ctx": lax.rem(me + n - shift_of(u, p), n)},
        )

    fetch_gate(0).start()
    fetch_down(0).start()
    barrier = pltpu.get_barrier_semaphore()
    for shift in range(1, n):
        pl.semaphore_signal(
            barrier, inc=1, device_id={"ctx": lax.rem(me + shift, n)}, device_id_type=MESH
        )
    pl.semaphore_signal(barrier, inc=1, device_id={"exp": 1 - exp}, device_id_type=MESH)
    pl.semaphore_signal(barrier, inc=1, device_id={"tp": 1 - tp}, device_id_type=MESH)
    pl.semaphore_wait(barrier, n + 1)
    for u, p in away:
        if u == 0:
            go(u, p).start()
    for u, p in here:
        rows[u, tp, p * C : (p + 1) * C] = tiles[u, p * C : (p + 1) * C]

    def receive(u):
        for v, p in away:
            if v == u:
                go(v, p).wait_recv()
        hand_over(u).start()
        for v, p in away:
            if v == u + 1:
                go(v, p).start()
        hand_over(u).wait_recv()

    def finish(u):
        far = pl.ds(pl.multiple_of((1 - tp) * half, 128), half)
        near = pl.ds(pl.multiple_of(tp * half, 128), half)
        swap_out[u] = acc[:, far].astype(jnp.bfloat16)
        swap(u).start()
        swap(u).wait_recv()
        back[u] = (acc[:, near] + swap_in[u].astype(jnp.float32)).astype(jnp.bfloat16)
        for v, p in away:
            if v == u:
                give(v, p).start()

    def step(k, carry):
        @pl.when(k < total)
        def _():
            e = k // pieces
            for u in range(units):
                pl.when(k == u * pieces)(lambda u=u: receive(u))

            @pl.when(k + 1 < total)
            def _():
                fetch_gate(k + 1).start()

            fetch_gate(k).wait()
            product = jnp.dot(
                rows[e, 0], gate_buf[k % 2, :half], preferred_element_type=jnp.float32
            ) + jnp.dot(rows[e, 1], gate_buf[k % 2, half:], preferred_element_type=jnp.float32)
            part[k] = product.astype(jnp.bfloat16)
            cross(k).start()

        @pl.when(k >= LAG)
        def _():
            j = k - LAG
            e = j // pieces

            @pl.when(j + 1 < total)
            def _():
                fetch_down(j + 1).start()

            cross(j).wait_recv()
            pre_act = part[j].astype(jnp.float32) + came[j].astype(jnp.float32)
            hidden = jax.nn.silu(pre_act).astype(jnp.bfloat16)
            fetch_down(j).wait()
            product = jnp.dot(hidden, down_buf[j % 2], preferred_element_type=jnp.float32)

            @pl.when(j % pieces == 0)
            def _():
                acc[...] = product

            @pl.when(j % pieces != 0)
            def _():
                acc[...] += product

            for u in range(units):
                pl.when(j == (u + 1) * pieces - 1)(lambda u=u: finish(u))

        return carry

    lax.fori_loop(0, total + LAG, step, 0)
    for u, p in here:
        out[u, p * C : (p + 1) * C] = back[u, p * C : (p + 1) * C]
    for u, p in away:
        give(u, p).wait_recv()
        out[u, p * C : (p + 1) * C] = landed[u, p * C : (p + 1) * C]

    def drain(k, carry):
        cross(k).wait_send()
        return carry

    lax.fori_loop(0, total, drain, 0)
    for u in range(units):
        hand_over(u).wait_send()
        swap(u).wait_send()
    for u, p in away:
        go(u, p).wait_send()
        give(u, p).wait_send()


def run_experts(tiles, gate, down, n, held):
    depth, units = gate.shape
    pieces = units // held // WIDTH
    parts = 2 * held
    total = parts * pieces
    count, half = tiles.shape[1], tiles.shape[2]
    wide = down.shape[1]
    dma = pltpu.SemaphoreType.DMA
    return pl.pallas_call(
        lambda *refs: expert_kernel(n, held, pieces, *refs),
        out_shape=jax.ShapeDtypeStruct((parts, count, wide // 2), jnp.bfloat16),
        in_specs=[
            pl.BlockSpec(memory_space=pltpu.VMEM),
            pl.BlockSpec(memory_space=pl.ANY),
            pl.BlockSpec(memory_space=pl.ANY),
        ],
        out_specs=pl.BlockSpec(memory_space=pltpu.VMEM),
        scratch_shapes=[
            pltpu.VMEM((parts, 2, count, half), jnp.bfloat16),
            pltpu.VMEM((2, depth, WIDTH), jnp.bfloat16),
            pltpu.VMEM((2, WIDTH, wide), jnp.bfloat16),
            pltpu.VMEM((total, count, WIDTH), jnp.bfloat16),
            pltpu.VMEM((total, count, WIDTH), jnp.bfloat16),
            pltpu.VMEM((count, wide), jnp.float32),
            pltpu.VMEM((parts, count, wide // 2), jnp.bfloat16),
            pltpu.VMEM((parts, count, wide // 2), jnp.bfloat16),
            pltpu.VMEM((parts, count, wide // 2), jnp.bfloat16),
            pltpu.VMEM((parts, count, wide // 2), jnp.bfloat16),
            dma((2,)), dma((2,)),
            dma((parts, n // 2)), dma((parts, n // 2)),
            dma((parts,)), dma((parts,)),
            dma((total,)), dma((total,)),
            dma((parts,)), dma((parts,)),
            dma((parts, n // 2)), dma((parts, n // 2)),
        ],
        compiler_params=pltpu.CompilerParams(
            collective_id=0, has_side_effects=True, vmem_limit_bytes=48 * 2**20
        ),
        cost_estimate=pl.CostEstimate(
            flops=8 * held * count * depth * units // held, bytes_accessed=8 * depth * units,
            transcendentals=0,
        ),
    )(tiles, gate, down)


def gather_kernel(n, pair, out, send_sem, recv_sem):
    me = lax.axis_index("ctx")
    count = pair.shape[0]

    def hop(shift):
        return pltpu.make_async_remote_copy(
            src_ref=pair, dst_ref=out.at[pl.ds(shift * count, count)],
            send_sem=send_sem.at[shift], recv_sem=recv_sem.at[shift],
            device_id={"ctx": lax.rem(me + shift, n)}, device_id_type=MESH,
        )

    barrier = pltpu.get_barrier_semaphore()
    for shift in range(1, n):
        pl.semaphore_signal(
            barrier, inc=1, device_id={"ctx": lax.rem(me + shift, n)}, device_id_type=MESH
        )
    pl.semaphore_wait(barrier, n - 1)
    for shift in range(1, n):
        pl.when(me + shift < n)(lambda shift=shift: hop(shift).start())
    out[:count] = pair[...]

    def blank(shift):
        out[shift * count : (shift + 1) * count] = jnp.zeros(pair.shape, pair.dtype)

    for shift in range(1, n):
        pl.when(me < shift)(lambda shift=shift: blank(shift))
        pl.when(me >= shift)(lambda shift=shift: hop(shift).wait_recv())
        pl.when(me + shift < n)(lambda shift=shift: hop(shift).wait_send())


def gather_earlier(pair, n):
    return pl.pallas_call(
        lambda *refs: gather_kernel(n, *refs),
        out_shape=jax.ShapeDtypeStruct((n * pair.shape[0], pair.shape[1]), pair.dtype),
        in_specs=[pl.BlockSpec(memory_space=pltpu.VMEM)],
        out_specs=pl.BlockSpec(memory_space=pltpu.VMEM),
        scratch_shapes=[pltpu.SemaphoreType.DMA((n,)), pltpu.SemaphoreType.DMA((n,))],
        compiler_params=pltpu.CompilerParams(collective_id=1, has_side_effects=True),
    )(pair)


def per_device(
    query_rows,
    key_rows,
    value_rows,
    residual,
    norm_gain,
    router_weight,
    expert_ids,
    gate_weight,
    down_weight,
):
    ctx_count = lax.axis_size("ctx")
    exp_count = lax.axis_size("exp")
    tp_count = lax.axis_size("tp")
    tp_index = lax.axis_index("tp")
    row_count = query_rows.shape[0]
    kv_local = key_rows.shape[1] // HD
    query_local = query_rows.shape[1] // HD
    group_size = QH // KVH
    assert group_size % query_local == 0 and tp_count == 2
    owner = (tp_index * query_local) // group_size
    first_row = lax.axis_index("ctx") * row_count
    query_pos = first_row + jnp.arange(row_count, dtype=jnp.int32)
    query_heads = query_rows.reshape(row_count, query_local, HD)

    def own_head(rows):
        return lax.dynamic_slice_in_dim(rows, owner * HD, HD, axis=1)

    pair = jnp.concatenate([own_head(key_rows), own_head(value_rows)], axis=1)
    direct = ctx_count <= 4 and E % ctx_count == 0
    if direct:
        pair = gather_earlier(pair, ctx_count)
        column = jnp.arange(pair.shape[0], dtype=jnp.int32)
        key_pos = first_row + column - 2 * (column // row_count) * row_count
        visible = (query_pos[:, None] >= key_pos[None, :]) & (key_pos >= 0)[None, :]
    else:
        pair = lax.all_gather(pair, "ctx", axis=0, tiled=True)
        visible = query_pos[:, None] >= jnp.arange(pair.shape[0], dtype=jnp.int32)[None, :]
    key_head, value_head = pair[:, :HD], pair[:, HD:]
    scores = jnp.einsum(
        "tqd,sd->qts", query_heads, key_head, preferred_element_type=jnp.float32
    ) * (1.0 / math.sqrt(HD))
    scores = jnp.where(visible[None], scores, floor_score)
    weights = jnp.exp(scores - jnp.max(scores, axis=-1, keepdims=True))
    run_total = jnp.sum(weights, axis=-1, keepdims=True)
    accumulated = jnp.einsum(
        "qts,sd->qtd",
        weights.astype(jnp.bfloat16),
        value_head,
        preferred_element_type=jnp.float32,
    )
    attended = jnp.transpose(accumulated / run_total, (1, 0, 2)).reshape(row_count, -1)
    mixed_in = residual.astype(jnp.float32) + attended
    scaled = mixed_in * norm_gain[None, :]
    square_sum = jnp.sum(mixed_in * mixed_in, axis=1)
    logit_part = jnp.dot(scaled, router_weight, precision=highest)
    ways = exp_count * tp_count
    if ways == 4:
        stats = jnp.concatenate([logit_part, square_sum[:, None]], axis=1).T
        for flip in (1, 2):
            stats = stats + lax.ppermute(stats, ("exp", "tp"), [(j, j ^ flip) for j in range(ways)])
        logit_part, square_sum = stats[:E].T, stats[E]
    else:
        square_sum, logit_part = lax.psum((square_sum, logit_part), ("exp", "tp"))
    inv_rms = lax.rsqrt(square_sum / (QH * HD) + epsilon)
    moe_half = (scaled * inv_rms[:, None]).astype(jnp.bfloat16)
    logits = logit_part * inv_rms[:, None]
    expert_range = jnp.arange(E, dtype=jnp.int32)
    chosen_hot = expert_ids[:, :, None] == expert_range[None, None, :]
    picked = jnp.sum(jnp.where(chosen_hot, logits[:, None, :], 0.0), axis=2)
    gate_pair = jnp.stack(
        [jax.nn.sigmoid(picked[:, 0] - picked[:, 1]), jax.nn.sigmoid(picked[:, 1] - picked[:, 0])],
        axis=1,
    )
    flat_ids = expert_ids.reshape(-1)
    flat_hot = (flat_ids[:, None] == expert_range[None, :]).astype(jnp.int32)
    slot_index = jnp.sum((jnp.cumsum(flat_hot, axis=0) - flat_hot) * flat_hot, axis=1)
    ctx_sharing = max(1, ctx_count // E)
    experts_held = max(1, E // ctx_count)
    kernel_path = (
        direct
        and exp_count == 2
        and ctx_count % 2 == 0
        and gate_weight.shape[2] // experts_held % WIDTH == 0
    )
    if direct:
        away = (flat_ids // experts_held - lax.axis_index("ctx") + ctx_count) % ctx_count
        local = flat_ids % experts_held
        if kernel_path:
            away = (away + (local == experts_held - 1) * (ctx_count // 2)) % ctx_count
        tile_index = local * ctx_count + away
    else:
        tile_index = (flat_ids % experts_held) * (E // experts_held) + flat_ids // experts_held
    tile_row = (tile_index * C + slot_index).reshape(row_count, 2)
    tile_range = jnp.arange(E * C, dtype=jnp.int32)
    tile_hot = tile_row[:, :, None] == tile_range[None, None, :]
    combine_matrix = jnp.sum(jnp.where(tile_hot, gate_pair[:, :, None], 0.0), axis=1)
    dispatch_matrix = jnp.transpose(jnp.any(tile_hot, axis=1)).astype(jnp.bfloat16)
    send_tiles = jnp.dot(dispatch_matrix, moe_half, preferred_element_type=jnp.float32).astype(
        jnp.bfloat16
    )
    send_tiles = send_tiles.reshape(experts_held, E // experts_held, C, -1)

    if kernel_path:
        returned = run_experts(
            send_tiles.reshape(2 * experts_held, ctx_count // 2 * C, -1),
            gate_weight.reshape(gate_weight.shape[0], -1),
            down_weight.reshape(-1, down_weight.shape[2]),
            ctx_count,
            experts_held,
        )
        moe_mine = jnp.dot(
            combine_matrix,
            returned.reshape(E * C, -1).astype(jnp.float32),
            precision=highest,
        )
        return (mixed_in + moe_mine).astype(jnp.bfloat16)

    def exchange(tiles, sign):
        if not direct:
            return lax.all_to_all(tiles, "ctx", split_axis=0, concat_axis=0, tiled=True)
        moved = [tiles[0]]
        for shift in range(1, ctx_count):
            turned = [(j, (j + sign * shift) % ctx_count) for j in range(ctx_count)]
            moved.append(lax.ppermute(tiles[shift], "ctx", turned))
        return jnp.stack(moved)

    hidden_width = gate_weight.shape[2] // experts_held
    pieces = max(1, min(PIECES, hidden_width // 512))
    piece = hidden_width // pieces
    halves = [
        exchange(jnp.repeat(send_tiles[e], ctx_sharing, axis=0), 1).reshape(ctx_count * C, -1)
        for e in range(experts_held)
    ]
    came = []
    sums = []
    for e in range(experts_held):
        half = halves[e]
        if came:
            half, came[0] = lax.optimization_barrier((half, came[0]))
        arrived = lax.all_gather(half, "tp", axis=1, tiled=True)
        for i in range(pieces):
            low = e * hidden_width + i * piece
            if len(came) >= 2:
                arrived, came[-2] = lax.optimization_barrier((arrived, came[-2]))
            part = jnp.dot(
                arrived,
                gate_weight[:, 0, low : low + piece],
                preferred_element_type=jnp.float32,
            ).astype(jnp.bfloat16)
            others = []
            for shift in range(1, exp_count):
                turned = [(j, (j + shift) % exp_count) for j in range(exp_count)]
                others.append(lax.ppermute(part, "exp", turned))
            came.append(others)
            sums.append(part)

    def total_of(k):
        return sum([p.astype(jnp.float32) for p in came[k]], sums[k].astype(jnp.float32))

    width_out = down_weight.shape[2] // tp_count
    moe_mine = 0.0
    combine_parts = combine_matrix.reshape(row_count, experts_held, -1)
    for e in range(experts_held):
        out = 0.0
        for i in range(pieces):
            low = e * hidden_width + i * piece
            hidden = jax.nn.silu(total_of(e * pieces + i)).astype(jnp.bfloat16)
            out = out + jnp.dot(
                hidden, down_weight[0, low : low + piece], preferred_element_type=jnp.float32
            )
        low_half, high_half = out[:, :width_out], out[:, width_out:]
        mine = jnp.where(tp_index == 0, low_half, high_half)
        other = jnp.where(tp_index == 0, high_half, low_half).astype(jnp.bfloat16)
        swapped = lax.ppermute(other, "tp", [(0, 1), (1, 0)])
        core_summed = (mine + swapped.astype(jnp.float32)).astype(jnp.bfloat16)
        returned = exchange(core_summed.reshape(ctx_count, C, width_out), -1).astype(jnp.float32)
        summed = jnp.sum(returned.reshape(-1, ctx_sharing, C, width_out), axis=1)
        moe_mine = moe_mine + jnp.dot(
            combine_parts[:, e],
            summed.reshape(-1, width_out),
            precision=highest,
        )
    return (mixed_in + moe_mine).astype(jnp.bfloat16)


def solution(mesh):
    return jax.shard_map(
        per_device,
        mesh=mesh,
        in_specs=(
            P(("groups", "ctx"), ("exp", "tp")),
            P(("groups", "ctx"), "exp"),
            P(("groups", "ctx"), "exp"),
            P(("groups", "ctx"), ("exp", "tp")),
            P(("exp", "tp")),
            P(("exp", "tp"), None),
            P(("groups", "ctx"), None),
            P("exp", "tp", "ctx"),
            P("tp", "ctx", "exp"),
        ),
        out_specs=P(("groups", "ctx"), ("exp", "tp")),
        check_vma=False,
    )
```

```python
import math

import jax
import jax.numpy as jnp
from jax import lax
from jax.experimental import pallas as pl
from jax.experimental.pallas import tpu as pltpu
from jax.sharding import PartitionSpec as P

HD = 128
QH = 24
KVH = 4
E = 8
C = 48
PIECES = 4


epsilon = 1e-05
highest = lax.Precision.HIGHEST
floor_score = -1e30


MESH = pl.DeviceIdType.MESH
WIDTH = 1024
LAG = 3


def expert_kernel(
    n, held, pieces, tiles, gate, down, out,
    rows, gate_buf, down_buf, part, came, acc, swap_out, swap_in, back, landed,
    gate_sem, down_sem, go_send, go_recv, pass_send, pass_recv, x_send, x_recv,
    swap_send, swap_recv, back_send, back_recv,
):
    me, exp, tp = lax.axis_index("ctx"), lax.axis_index("exp"), lax.axis_index("tp")
    units = 2 * held
    per = n // 2
    total = units * pieces
    half = rows.shape[3]

    def shift_of(u, p):
        spot = (u % 2) * per + p
        return (spot + per) % n if u // 2 == held - 1 else spot

    every = [(u, p) for u in range(units) for p in range(per)]
    away = [(u, p) for u, p in every if shift_of(u, p)]
    here = [(u, p) for u, p in every if not shift_of(u, p)]

    def block_of(k):
        place = (k // pieces // 2) * pieces + k % pieces
        return pl.ds(pl.multiple_of(place * WIDTH, WIDTH), WIDTH)

    def fetch_gate(k):
        return pltpu.make_async_copy(gate.at[:, block_of(k)], gate_buf.at[k % 2], gate_sem.at[k % 2])

    def fetch_down(k):
        return pltpu.make_async_copy(down.at[block_of(k)], down_buf.at[k % 2], down_sem.at[k % 2])

    def remote(src, dst, send, recv, where):
        return pltpu.make_async_remote_copy(
            src_ref=src, dst_ref=dst, send_sem=send, recv_sem=recv,
            device_id=where, device_id_type=MESH,
        )

    def go(u, p):
        spot = pl.ds(p * C, C)
        return remote(
            tiles.at[u, spot], rows.at[u, tp, spot], go_send.at[u, p], go_recv.at[u, p],
            {"ctx": lax.rem(me + shift_of(u, p), n)},
        )

    def hand_over(e):
        return remote(
            rows.at[e, tp], rows.at[e, tp], pass_send.at[e], pass_recv.at[e], {"tp": 1 - tp}
        )

    def cross(k):
        return remote(part.at[k], came.at[k], x_send.at[k], x_recv.at[k], {"exp": 1 - exp})

    def swap(e):
        return remote(swap_out.at[e], swap_in.at[e], swap_send.at[e], swap_recv.at[e], {"tp": 1 - tp})

    def give(u, p):
        spot = pl.ds(p * C, C)
        return remote(
            back.at[u, spot], landed.at[u, spot], back_send.at[u, p], back_recv.at[u, p],
            {"ctx": lax.rem(me + n - shift_of(u, p), n)},
        )

    fetch_gate(0).start()
    fetch_down(0).start()
    barrier = pltpu.get_barrier_semaphore()
    for shift in range(1, n):
        pl.semaphore_signal(
            barrier, inc=1, device_id={"ctx": lax.rem(me + shift, n)}, device_id_type=MESH
        )
    pl.semaphore_signal(barrier, inc=1, device_id={"exp": 1 - exp}, device_id_type=MESH)
    pl.semaphore_signal(barrier, inc=1, device_id={"tp": 1 - tp}, device_id_type=MESH)
    pl.semaphore_wait(barrier, n + 1)
    for u, p in away:
        if u == 0:
            go(u, p).start()
    for u, p in here:
        rows[u, tp, p * C : (p + 1) * C] = tiles[u, p * C : (p + 1) * C]

    def receive(u):
        for v, p in away:
            if v == u:
                go(v, p).wait_recv()
        hand_over(u).start()
        for v, p in away:
            if v == u + 1:
                go(v, p).start()
        hand_over(u).wait_recv()

    def finish(u):
        far = pl.ds(pl.multiple_of((1 - tp) * half, 128), half)
        near = pl.ds(pl.multiple_of(tp * half, 128), half)
        swap_out[u] = acc[:, far].astype(jnp.bfloat16)
        swap(u).start()
        swap(u).wait_recv()
        back[u] = (acc[:, near] + swap_in[u].astype(jnp.float32)).astype(jnp.bfloat16)
        for v, p in away:
            if v == u:
                give(v, p).start()

    def step(k, carry):
        @pl.when(k < total)
        def _():
            e = k // pieces
            for u in range(units):
                pl.when(k == u * pieces)(lambda u=u: receive(u))

            @pl.when(k + 1 < total)
            def _():
                fetch_gate(k + 1).start()

            fetch_gate(k).wait()
            product = jnp.dot(
                rows[e, 0], gate_buf[k % 2, :half], preferred_element_type=jnp.float32
            ) + jnp.dot(rows[e, 1], gate_buf[k % 2, half:], preferred_element_type=jnp.float32)
            part[k] = product.astype(jnp.bfloat16)
            cross(k).start()

        @pl.when(k >= LAG)
        def _():
            j = k - LAG
            e = j // pieces

            @pl.when(j + 1 < total)
            def _():
                fetch_down(j + 1).start()

            cross(j).wait_recv()
            pre_act = part[j].astype(jnp.float32) + came[j].astype(jnp.float32)
            hidden = jax.nn.silu(pre_act).astype(jnp.bfloat16)
            fetch_down(j).wait()
            product = jnp.dot(hidden, down_buf[j % 2], preferred_element_type=jnp.float32)

            @pl.when(j % pieces == 0)
            def _():
                acc[...] = product

            @pl.when(j % pieces != 0)
            def _():
                acc[...] += product

            for u in range(units):
                pl.when(j == (u + 1) * pieces - 1)(lambda u=u: finish(u))

        return carry

    lax.fori_loop(0, total + LAG, step, 0)
    for u, p in here:
        out[u, p * C : (p + 1) * C] = back[u, p * C : (p + 1) * C]
    for u, p in away:
        give(u, p).wait_recv()
        out[u, p * C : (p + 1) * C] = landed[u, p * C : (p + 1) * C]

    def drain(k, carry):
        cross(k).wait_send()
        return carry

    lax.fori_loop(0, total, drain, 0)
    for u in range(units):
        hand_over(u).wait_send()
        swap(u).wait_send()
    for u, p in away:
        go(u, p).wait_send()
        give(u, p).wait_send()


def run_experts(tiles, gate, down, n, held):
    depth, units = gate.shape
    pieces = units // held // WIDTH
    parts = 2 * held
    total = parts * pieces
    count, half = tiles.shape[1], tiles.shape[2]
    wide = down.shape[1]
    dma = pltpu.SemaphoreType.DMA
    return pl.pallas_call(
        lambda *refs: expert_kernel(n, held, pieces, *refs),
        out_shape=jax.ShapeDtypeStruct((parts, count, wide // 2), jnp.bfloat16),
        in_specs=[
            pl.BlockSpec(memory_space=pltpu.VMEM),
            pl.BlockSpec(memory_space=pl.ANY),
            pl.BlockSpec(memory_space=pl.ANY),
        ],
        out_specs=pl.BlockSpec(memory_space=pltpu.VMEM),
        scratch_shapes=[
            pltpu.VMEM((parts, 2, count, half), jnp.bfloat16),
            pltpu.VMEM((2, depth, WIDTH), jnp.bfloat16),
            pltpu.VMEM((2, WIDTH, wide), jnp.bfloat16),
            pltpu.VMEM((total, count, WIDTH), jnp.bfloat16),
            pltpu.VMEM((total, count, WIDTH), jnp.bfloat16),
            pltpu.VMEM((count, wide), jnp.float32),
            pltpu.VMEM((parts, count, wide // 2), jnp.bfloat16),
            pltpu.VMEM((parts, count, wide // 2), jnp.bfloat16),
            pltpu.VMEM((parts, count, wide // 2), jnp.bfloat16),
            pltpu.VMEM((parts, count, wide // 2), jnp.bfloat16),
            dma((2,)), dma((2,)),
            dma((parts, n // 2)), dma((parts, n // 2)),
            dma((parts,)), dma((parts,)),
            dma((total,)), dma((total,)),
            dma((parts,)), dma((parts,)),
            dma((parts, n // 2)), dma((parts, n // 2)),
        ],
        compiler_params=pltpu.CompilerParams(
            collective_id=0, has_side_effects=True, vmem_limit_bytes=48 * 2**20
        ),
        cost_estimate=pl.CostEstimate(
            flops=8 * held * count * depth * units // held, bytes_accessed=8 * depth * units,
            transcendentals=0,
        ),
    )(tiles, gate, down)


def per_device(
    query_rows,
    key_rows,
    value_rows,
    residual,
    norm_gain,
    router_weight,
    expert_ids,
    gate_weight,
    down_weight,
):
    ctx_count = lax.axis_size("ctx")
    exp_count = lax.axis_size("exp")
    tp_count = lax.axis_size("tp")
    tp_index = lax.axis_index("tp")
    row_count = query_rows.shape[0]
    kv_local = key_rows.shape[1] // HD
    query_local = query_rows.shape[1] // HD
    group_size = QH // KVH
    assert group_size % query_local == 0 and tp_count == 2
    owner = (tp_index * query_local) // group_size
    first_row = lax.axis_index("ctx") * row_count
    query_pos = first_row + jnp.arange(row_count, dtype=jnp.int32)
    query_heads = query_rows.reshape(row_count, query_local, HD)

    def own_head(rows):
        return lax.dynamic_slice_in_dim(rows, owner * HD, HD, axis=1)

    pair = jnp.concatenate([own_head(key_rows), own_head(value_rows)], axis=1)
    direct = ctx_count <= 4 and E % ctx_count == 0
    if direct:
        pieces_kv = [pair]
        for shift in range(1, ctx_count):
            later = [(j, j + shift) for j in range(ctx_count - shift)]
            pieces_kv.append(lax.ppermute(pair, "ctx", later))
        pair = jnp.concatenate(pieces_kv, axis=0)
        column = jnp.arange(pair.shape[0], dtype=jnp.int32)
        key_pos = first_row + column - 2 * (column // row_count) * row_count
        visible = (query_pos[:, None] >= key_pos[None, :]) & (key_pos >= 0)[None, :]
    else:
        pair = lax.all_gather(pair, "ctx", axis=0, tiled=True)
        visible = query_pos[:, None] >= jnp.arange(pair.shape[0], dtype=jnp.int32)[None, :]
    key_head, value_head = pair[:, :HD], pair[:, HD:]
    scores = jnp.einsum(
        "tqd,sd->qts", query_heads, key_head, preferred_element_type=jnp.float32
    ) * (1.0 / math.sqrt(HD))
    scores = jnp.where(visible[None], scores, floor_score)
    weights = jnp.exp(scores - jnp.max(scores, axis=-1, keepdims=True))
    run_total = jnp.sum(weights, axis=-1, keepdims=True)
    accumulated = jnp.einsum(
        "qts,sd->qtd",
        weights.astype(jnp.bfloat16),
        value_head,
        preferred_element_type=jnp.float32,
    )
    attended = jnp.transpose(accumulated / run_total, (1, 0, 2)).reshape(row_count, -1)
    mixed_in = residual.astype(jnp.float32) + attended
    scaled = mixed_in * norm_gain[None, :]
    square_sum = jnp.sum(mixed_in * mixed_in, axis=1)
    logit_part = jnp.dot(scaled, router_weight, precision=highest)
    ways = exp_count * tp_count
    if ways == 4:
        stats = jnp.concatenate([logit_part, square_sum[:, None]], axis=1).T
        others = [
            lax.ppermute(stats, ("exp", "tp"), [(j, j ^ flip) for j in range(ways)])
            for flip in (1, 2, 3)
        ]
        stats = (stats + others[0]) + (others[1] + others[2])
        logit_part, square_sum = stats[:E].T, stats[E]
    else:
        square_sum, logit_part = lax.psum((square_sum, logit_part), ("exp", "tp"))
    inv_rms = lax.rsqrt(square_sum / (QH * HD) + epsilon)
    moe_half = (scaled * inv_rms[:, None]).astype(jnp.bfloat16)
    logits = logit_part * inv_rms[:, None]
    expert_range = jnp.arange(E, dtype=jnp.int32)
    chosen_hot = expert_ids[:, :, None] == expert_range[None, None, :]
    picked = jnp.sum(jnp.where(chosen_hot, logits[:, None, :], 0.0), axis=2)
    gate_pair = jnp.stack(
        [jax.nn.sigmoid(picked[:, 0] - picked[:, 1]), jax.nn.sigmoid(picked[:, 1] - picked[:, 0])],
        axis=1,
    )
    flat_ids = expert_ids.reshape(-1)
    flat_hot = (flat_ids[:, None] == expert_range[None, :]).astype(jnp.int32)
    slot_index = jnp.sum((jnp.cumsum(flat_hot, axis=0) - flat_hot) * flat_hot, axis=1)
    ctx_sharing = max(1, ctx_count // E)
    experts_held = max(1, E // ctx_count)
    kernel_path = (
        direct
        and exp_count == 2
        and ctx_count % 2 == 0
        and gate_weight.shape[2] // experts_held % WIDTH == 0
    )
    if direct:
        away = (flat_ids // experts_held - lax.axis_index("ctx") + ctx_count) % ctx_count
        local = flat_ids % experts_held
        if kernel_path:
            away = (away + (local == experts_held - 1) * (ctx_count // 2)) % ctx_count
        tile_index = local * ctx_count + away
    else:
        tile_index = (flat_ids % experts_held) * (E // experts_held) + flat_ids // experts_held
    tile_row = (tile_index * C + slot_index).reshape(row_count, 2)
    tile_range = jnp.arange(E * C, dtype=jnp.int32)
    tile_hot = tile_row[:, :, None] == tile_range[None, None, :]
    combine_matrix = jnp.sum(jnp.where(tile_hot, gate_pair[:, :, None], 0.0), axis=1)
    dispatch_matrix = jnp.transpose(jnp.any(tile_hot, axis=1)).astype(jnp.bfloat16)
    send_tiles = jnp.dot(dispatch_matrix, moe_half, preferred_element_type=jnp.float32).astype(
        jnp.bfloat16
    )
    send_tiles = send_tiles.reshape(experts_held, E // experts_held, C, -1)

    if kernel_path:
        returned = run_experts(
            send_tiles.reshape(2 * experts_held, ctx_count // 2 * C, -1),
            gate_weight.reshape(gate_weight.shape[0], -1),
            down_weight.reshape(-1, down_weight.shape[2]),
            ctx_count,
            experts_held,
        )
        moe_mine = jnp.dot(
            combine_matrix,
            returned.reshape(E * C, -1).astype(jnp.float32),
            precision=highest,
        )
        return (mixed_in + moe_mine).astype(jnp.bfloat16)

    def exchange(tiles, sign):
        if not direct:
            return lax.all_to_all(tiles, "ctx", split_axis=0, concat_axis=0, tiled=True)
        moved = [tiles[0]]
        for shift in range(1, ctx_count):
            turned = [(j, (j + sign * shift) % ctx_count) for j in range(ctx_count)]
            moved.append(lax.ppermute(tiles[shift], "ctx", turned))
        return jnp.stack(moved)

    hidden_width = gate_weight.shape[2] // experts_held
    pieces = max(1, min(PIECES, hidden_width // 512))
    piece = hidden_width // pieces
    halves = [
        exchange(jnp.repeat(send_tiles[e], ctx_sharing, axis=0), 1).reshape(ctx_count * C, -1)
        for e in range(experts_held)
    ]
    came = []
    sums = []
    for e in range(experts_held):
        half = halves[e]
        if came:
            half, came[0] = lax.optimization_barrier((half, came[0]))
        arrived = lax.all_gather(half, "tp", axis=1, tiled=True)
        for i in range(pieces):
            low = e * hidden_width + i * piece
            if len(came) >= 2:
                arrived, came[-2] = lax.optimization_barrier((arrived, came[-2]))
            part = jnp.dot(
                arrived,
                gate_weight[:, 0, low : low + piece],
                preferred_element_type=jnp.float32,
            ).astype(jnp.bfloat16)
            others = []
            for shift in range(1, exp_count):
                turned = [(j, (j + shift) % exp_count) for j in range(exp_count)]
                others.append(lax.ppermute(part, "exp", turned))
            came.append(others)
            sums.append(part)

    def total_of(k):
        return sum([p.astype(jnp.float32) for p in came[k]], sums[k].astype(jnp.float32))

    width_out = down_weight.shape[2] // tp_count
    moe_mine = 0.0
    combine_parts = combine_matrix.reshape(row_count, experts_held, -1)
    for e in range(experts_held):
        out = 0.0
        for i in range(pieces):
            low = e * hidden_width + i * piece
            hidden = jax.nn.silu(total_of(e * pieces + i)).astype(jnp.bfloat16)
            out = out + jnp.dot(
                hidden, down_weight[0, low : low + piece], preferred_element_type=jnp.float32
            )
        low_half, high_half = out[:, :width_out], out[:, width_out:]
        mine = jnp.where(tp_index == 0, low_half, high_half)
        other = jnp.where(tp_index == 0, high_half, low_half).astype(jnp.bfloat16)
        swapped = lax.ppermute(other, "tp", [(0, 1), (1, 0)])
        core_summed = (mine + swapped.astype(jnp.float32)).astype(jnp.bfloat16)
        returned = exchange(core_summed.reshape(ctx_count, C, width_out), -1).astype(jnp.float32)
        summed = jnp.sum(returned.reshape(-1, ctx_sharing, C, width_out), axis=1)
        moe_mine = moe_mine + jnp.dot(
            combine_parts[:, e],
            summed.reshape(-1, width_out),
            precision=highest,
        )
    return (mixed_in + moe_mine).astype(jnp.bfloat16)


def solution(mesh):
    return jax.shard_map(
        per_device,
        mesh=mesh,
        in_specs=(
            P(("groups", "ctx"), ("exp", "tp")),
            P(("groups", "ctx"), "exp"),
            P(("groups", "ctx"), "exp"),
            P(("groups", "ctx"), ("exp", "tp")),
            P(("exp", "tp")),
            P(("exp", "tp"), None),
            P(("groups", "ctx"), None),
            P("exp", "tp", "ctx"),
            P("tp", "ctx", "exp"),
        ),
        out_specs=P(("groups", "ctx"), ("exp", "tp")),
        check_vma=False,
    )
```
